512 devices in a mesh: dom: 128 (over z, x, y_lo), rep: 4 (over y_hi, core).
Axes of the slice: x: 4, y: 4 (y_hi: 2, y_lo: 2; y = y_hi * 2 + y_lo), z: 16, core: 2. Of those that a mesh axis runs over, the one named last changes fastest.
Arguments:
- entities: float32 [131072, 400], P(('dom', 'rep')), may hold values from -1.8 to 1.8
- ent_state: float32 [131072], P(('dom', 'rep')), may hold values from 0.01 to 0.1
- relations: float32 [2560, 400], P(('dom', 'rep')), may hold values from -3 to 3
- rel_state: float32 [2560], P(('dom', 'rep')), may hold values from 1 to 10
- src_rows: int32 [512, 256], P(('dom', 'rep')), may hold values from 0 to 255
- dst_rows: int32 [512, 256], P(('dom', 'rep')), may hold values from 0 to 1023
- rel_ids: int32 [512, 256], P(('dom', 'rep')), may hold values from 0 to 2559
- neg_src: int32 [512, 1000], P(('dom', 'rep')), may hold values from 0 to 255
- neg_dst: int32 [512, 1000], P(('dom', 'rep')), may hold values from 0 to 1023
- edge_count: int32 [512], P(('dom', 'rep')), may hold values from 64 to 256, as said below
Outputs:
- new_entities: float32 [131072, 400], P(('dom', 'rep'))
- new_ent_state: float32 [131072], P(('dom', 'rep'))
- new_relations: float32 [2560, 400], P(('dom', 'rep'))
- new_rel_state: float32 [2560], P(('dom', 'rep'))
The draws below stay inside these ranges and needn't reach their ends.
Inputs may be any that keep to these rules, and one draw needn't show every extreme that they name: `edge_count`: live edge slots of each device; some device fills all 256 slots.
All inputs are finite; a program needn't handle non-finite values.
Results may differ from the reference program's by a relative error of at most 0.0048.
Values may be sent and summed in bfloat16 or wider, within the bound.
A program may use at most 64 MiB of HBM per device.

```python
import math
import jax
import jax.numpy as jnp
from jax import lax

D = 400
NREL = 2560
NEG = 1000
ROWS = 256
EDGE_CAP = 256
DEV_ALL = 512
REL_DEV = 5
PART_ROWS = 1024
ENTITIES = 131072
N_DOM = 128
N_REP = 4


def draw_rel_ids(key, part):
    key = jax.random.fold_in(key, 3)
    first, second, third = jax.random.split(key, 3)
    owner = jnp.arange(DEV_ALL, dtype=jnp.int32)[:, None]
    local = owner * REL_DEV + jax.random.randint(first, (DEV_ALL, EDGE_CAP), 0, REL_DEV)
    spread = jax.random.randint(second, (DEV_ALL, EDGE_CAP), 0, NREL)
    pick = jax.random.randint(third, (DEV_ALL, EDGE_CAP), 0, 2)
    return jnp.where(pick == 1, local, spread).astype(jnp.int32)


def draw_edge_count(key, part):
    key = jax.random.fold_in(key, 5)
    first, second = jax.random.split(key, 2)
    counts = jax.random.randint(first, (DEV_ALL,), EDGE_CAP // 4, EDGE_CAP + 1)
    order = jax.random.permutation(second, DEV_ALL)
    counts = counts.at[order[0]].set(EDGE_CAP).at[order[1]].set(EDGE_CAP // 4)
    return counts.astype(jnp.int32)


def with_ends(drawn, key, smallest, top_value):
    dims = drawn.shape
    index_at = [jax.random.randint(jax.random.fold_in(key, axis), (), 0, dims[axis]) for axis in range(len(dims))]
    drawn = drawn.at[tuple(index_at)].set(smallest)
    longest = dims.index(max(dims))
    index_at[longest] = (index_at[longest] + 1) % dims[longest]
    return drawn.at[tuple(index_at)].set(top_value)


def shard_levels(rng, dims, shards, least, top_value):
    def one(axis_at, parts):
        steps = jax.random.uniform(jax.random.fold_in(jax.random.fold_in(rng, 6), axis_at), (parts,), jnp.float32, least / len(shards), top_value / len(shards))
        return jnp.repeat(jnp.exp(steps), dims[axis_at] // parts).reshape((-1,) + (1,) * (len(dims) - axis_at - 1))

    gain = one(*shards[0])
    for cut in shards[1:]:
        gain = gain * one(*cut)
    return gain


def normal_values(own_key, shape, scale, bound, pieces=(), kind=jnp.bfloat16):
    factor_of = shard_levels(own_key, shape, pieces, -0.22, 0.18) if pieces else 1.0
    result = jax.random.normal(own_key, shape, jnp.float32) * scale * factor_of
    return jnp.minimum(jnp.maximum(result, -bound), bound).astype(kind)


def setup_inputs(seed: int = 0) -> dict:
    key_list = jax.random.split(jax.random.key(seed), 11)
    entities = normal_values(key_list[0], (ENTITIES, D), 0.3, 1.8, ((0, 512),), jnp.float32)
    ent_state = jnp.clip(jnp.exp(math.log(0.1) - 2.3025851 * jax.random.uniform(key_list[1], (ENTITIES,), jnp.float32) ** shard_levels(key_list[1], (ENTITIES,), ((0, 512),), -0.2, 0.2)), 0.01, 0.1)
    relations = normal_values(key_list[2], (NREL, D), 0.5, 3.0, ((0, 512),), jnp.float32)
    rel_state = jnp.clip(jnp.exp(math.log(10.0) - 2.3025851 * jax.random.uniform(key_list[3], (NREL,), jnp.float32) ** shard_levels(key_list[3], (NREL,), ((0, 512),), -0.2, 0.2)), 1.0, 10.0)
    src_rows = with_ends(jax.random.randint(key_list[4], (DEV_ALL, EDGE_CAP), 0, ROWS), jax.random.fold_in(key_list[4], 1), 0, ROWS - 1).astype(jnp.int32)
    dst_rows = with_ends(jax.random.randint(key_list[5], (DEV_ALL, EDGE_CAP), 0, PART_ROWS), jax.random.fold_in(key_list[5], 1), 0, PART_ROWS - 1).astype(jnp.int32)
    rel_ids = draw_rel_ids(jax.random.fold_in(key_list[10], 71), 0)
    neg_src = with_ends(jax.random.randint(key_list[7], (DEV_ALL, NEG), 0, ROWS), jax.random.fold_in(key_list[7], 1), 0, ROWS - 1).astype(jnp.int32)
    neg_dst = with_ends(jax.random.randint(key_list[8], (DEV_ALL, NEG), 0, PART_ROWS), jax.random.fold_in(key_list[8], 1), 0, PART_ROWS - 1).astype(jnp.int32)
    edge_count = draw_edge_count(jax.random.fold_in(key_list[10], 71), 0)
    return {"entities": entities, "ent_state": ent_state, "relations": relations, "rel_state": rel_state, "src_rows": src_rows, "dst_rows": dst_rows, "rel_ids": rel_ids, "neg_src": neg_src, "neg_dst": neg_dst, "edge_count": edge_count}


def complex_mul(left, right):
    width = left.shape[-1] // 2
    left_re, left_im = (left[..., :width], left[..., width:])
    right_re, right_im = (right[..., :width], right[..., width:])
    return jnp.concatenate([left_re * right_re - left_im * right_im, left_re * right_im + left_im * right_re], -1)

def conjugate(values):
    width = values.shape[-1] // 2
    return jnp.concatenate([values[..., :width], -values[..., width:]], -1)

def bucket_grads(own_rows, part_rows, rel_table, src_idx, dst_idx, rel_idx, nsrc_idx, ndst_idx, count):
    slots = src_idx.shape[0]
    negatives = nsrc_idx.shape[0]
    sources = own_rows[src_idx].astype(jnp.float32)
    objects = part_rows[dst_idx].astype(jnp.float32)
    operators = rel_table[rel_idx].astype(jnp.float32)
    live = (jnp.arange(slots, dtype=jnp.int32) < count).astype(jnp.float32)
    queries = complex_mul(sources, operators)
    turned = complex_mul(conjugate(operators), objects)
    query_half = queries.astype(jnp.bfloat16)
    turned_half = turned.astype(jnp.bfloat16)
    neg_sources = own_rows[nsrc_idx]
    neg_objects = part_rows[ndst_idx]
    positive = lax.optimization_barrier(jnp.sum(queries * objects, -1))
    grad_pos = -live * jax.nn.sigmoid(-positive)
    dst_scores = jnp.dot(query_half, neg_objects.T, preferred_element_type=jnp.float32)
    src_scores = jnp.dot(turned_half, neg_sources.T, preferred_element_type=jnp.float32)
    grad_dst = (live[:, None] * jax.nn.sigmoid(dst_scores) / negatives).astype(jnp.bfloat16)
    grad_src = (live[:, None] * jax.nn.sigmoid(src_scores) / negatives).astype(jnp.bfloat16)
    d_query = grad_pos[:, None] * objects + jnp.dot(grad_dst, neg_objects, preferred_element_type=jnp.float32)
    d_turned = grad_pos[:, None] * sources + jnp.dot(grad_src, neg_sources, preferred_element_type=jnp.float32)
    d_negobj = jnp.dot(grad_dst.T, query_half, preferred_element_type=jnp.float32)
    d_negsrc = jnp.dot(grad_src.T, turned_half, preferred_element_type=jnp.float32)
    d_source = complex_mul(conjugate(operators), d_query) + grad_pos[:, None] * turned
    d_object = grad_pos[:, None] * queries + complex_mul(operators, d_turned)
    d_operator = complex_mul(conjugate(sources), d_query) + complex_mul(objects, conjugate(d_turned))
    src_term = jax.ops.segment_sum(d_source, src_idx, own_rows.shape[0]) + jax.ops.segment_sum(d_negsrc, nsrc_idx, own_rows.shape[0])
    dst_term = jax.ops.segment_sum(d_object, dst_idx, part_rows.shape[0]) + jax.ops.segment_sum(d_negobj, ndst_idx, part_rows.shape[0])
    rel_term = jax.ops.segment_sum(d_operator, rel_idx, rel_table.shape[0])
    return (src_term, dst_term.astype(jnp.bfloat16), rel_term)

def reference(entities, ent_state, relations, rel_state, src_rows, dst_rows, rel_ids, neg_src, neg_dst, edge_count):
    ent_half = entities.astype(jnp.bfloat16)
    rel_half = relations.astype(jnp.bfloat16)
    part_size = ROWS * N_REP

    def visit(carry, device):
        ent_acc, rel_acc = carry
        owner = device // N_REP
        target = (owner + N_DOM // 2) % N_DOM
        own_rows = lax.dynamic_slice_in_dim(ent_half, (device * ROWS).astype(jnp.int32), ROWS, 0)
        part_rows = lax.dynamic_slice_in_dim(ent_half, (target * part_size).astype(jnp.int32), part_size, 0)
        src_term, dst_term, rel_term = bucket_grads(own_rows, part_rows, rel_half, src_rows[device], dst_rows[device], rel_ids[device], neg_src[device], neg_dst[device], edge_count[device])
        start_own = (device * ROWS).astype(jnp.int32)
        old_own = lax.dynamic_slice_in_dim(ent_acc, start_own, ROWS, 0)
        ent_acc = lax.dynamic_update_slice_in_dim(ent_acc, old_own + src_term, start_own, 0)
        start_dst = (target * part_size).astype(jnp.int32)
        old_dst = lax.dynamic_slice_in_dim(ent_acc, start_dst, part_size, 0)
        ent_acc = lax.dynamic_update_slice_in_dim(ent_acc, old_dst + dst_term.astype(jnp.float32), start_dst, 0)
        return ((ent_acc, rel_acc + rel_term), None)
    start = (jnp.zeros(entities.shape, jnp.float32), jnp.zeros(relations.shape, jnp.float32))
    (ent_grad, rel_grad), _ = lax.scan(visit, start, jnp.arange(N_DOM * N_REP, dtype=jnp.int32))
    new_ent_state = ent_state + lax.optimization_barrier(jnp.mean(ent_grad * ent_grad, -1))
    new_entities = entities - 0.5 * ent_grad / jnp.sqrt(new_ent_state)[:, None]
    new_rel_state = rel_state + lax.optimization_barrier(jnp.mean(rel_grad * rel_grad, -1))
    new_relations = relations - 0.5 * rel_grad / jnp.sqrt(new_rel_state)[:, None]
    return (new_entities, new_ent_state, new_relations, new_rel_state)
```

```python
import jax
import jax.numpy as jnp
from jax import lax
from jax.experimental import pallas as pl
from jax.experimental.pallas import tpu as pltpu
from jax.sharding import PartitionSpec as P

Z, X, YL, YH, CORES = 16, 4, 2, 2, 2
Y = YL * YH
PI = X * Y
D = 400
HALF = D // 2
PAD = 512
ROWS = 256
EDGES = 256
NEG = 1000
NEG_PAD = 1024
REP = YH * CORES
REL_DEV = 5
TILE = 16
REL_ROWS = Z * TILE
CB = Z * REL_DEV
CHUNKS = 5
CH = D // CHUNKS
GROUP = min(4, PI)
GROUPS = PI // GROUP
STEP = 40
STEPS = HALF // STEP
SHIFT_PLANE = (PI * CORES).bit_length() - 1
SHIFT_CORE = CORES.bit_length() - 1
BF = jnp.bfloat16
F32 = jnp.float32
MESH = pl.DeviceIdType.MESH


def nn(a, b):
    return jnp.dot(a, b, preferred_element_type=F32)


def nt(a, b):
    return lax.dot_general(a, b, (((1,), (1,)), ((), ())), preferred_element_type=F32)


def iota(shape, dim):
    return lax.broadcasted_iota(jnp.int32, shape, dim)


def one_hot(cond):
    return jnp.where(cond, 1.0, 0.0).astype(BF)


def div5(v):
    return lax.shift_right_logical(v * 52429, 18)


def remote(src, dst, send, recv, peer):
    return pltpu.make_async_remote_copy(
        src_ref=src, dst_ref=dst, send_sem=send, recv_sem=recv, device_id=peer, device_id_type=MESH
    )


def kernel(
    ent, state, rel, rel_state, src_rows, dst_rows, rel_ids, neg_src, neg_dst, count,
    new_ent, new_state, new_rel, new_rel_state,
    eb, part, zt, g, tf, ohs, ohd, ohx, ohz, ohxt, ohzt, negs, cnts,
    sf, wf, of, qf, uf, dqf, dpf, dof, dsf, dwf,
    qb, qrow, urow, gmat, gs, dob, dwb, dwz,
    dest, dcr, ysend, yrecv, ezs, ezr, rblk, rcr, rpr, zsend, zrecv,
    zt_s, zt_r, e_s, e_r, y_s, y_r, c1_s, c1_r, c2_s, c2_r, p_s, p_r, g_s, g_r,
    dc_s, dc_r, dy_s, dy_r, dz_s, dz_r, rc_s, rc_r, rp_s, rp_r, rz_s, rz_r,
):
    dom = lax.axis_index("dom")
    rep = lax.axis_index("rep")
    z = dom // (X * YL)
    x = (dom // YL) % X
    yl = dom % YL
    yh = rep // CORES
    c = rep % CORES
    y = yh * YL + yl
    cm = 1 - c
    pi = (x * YL + yl) * YH + yh

    def device(dz, dx, dy, core):
        yy = (y + dy) % Y
        return {
            "dom": (((z + dz) % Z) * X + (x + dx) % X) * YL + yy % YL,
            "rep": (yy // YL) * CORES + core,
        }

    def plane_peer(n):
        return device(0, n // Y, n % Y, c)

    def plane_index(n):
        yy = (y + n % Y) % Y
        return (((x + n // Y) % X) * YL + yy % YL) * YH + yy // YL

    def plane_from(n):
        yy = (y + Y - n % Y) % Y
        return (((x + X - n // Y) % X) * YL + yy % YL) * YH + yy // YL

    mate = device(0, 0, 0, cm)
    across = device(0, 0, YL, c)
    far = device(Z // 2, 0, 0, c)

    barrier = pltpu.get_barrier_semaphore()

    @pl.loop(1, Z)
    def _(n):
        pl.semaphore_signal(barrier, inc=1, device_id=device(n, 0, 0, c), device_id_type=MESH)

    @pl.loop(1, PI)
    def _(n):
        pl.semaphore_signal(barrier, inc=1, device_id=plane_peer(n), device_id_type=MESH)

    pl.semaphore_signal(barrier, inc=1, device_id=mate, device_id_type=MESH)

    eb[0:D, :] = ent[...].astype(BF)
    lane = iota((REL_DEV, 128), 1)
    row5 = iota((REL_DEV, 128), 0)
    for k in range(3):
        tf[k * REL_DEV : (k + 1) * REL_DEV, :] = rel[:, k * 128 : (k + 1) * 128]
    spread16 = one_hot((iota((16, 128), 1) & 15) == iota((16, 128), 0))
    last = nn(rel[:, 384:400].astype(BF), spread16)
    last = jnp.where(lax.shift_right_logical(lane, 4) == row5, last, 0.0)
    tf[15:16, :] = jnp.sum(last, axis=0, keepdims=True)
    own_tile = pl.ds(pl.multiple_of(z * TILE, TILE), TILE)
    zt[own_tile, :] = tf[...].astype(BF)

    pl.semaphore_wait(barrier, (Z - 1) + (PI - 1) + 1)

    def tile_copy(n):
        return remote(zt.at[own_tile], zt.at[own_tile], zt_s.at[n], zt_r.at[n], device(n, 0, 0, c))

    @pl.loop(1, Z)
    def _(n):
        tile_copy(n).start()

    def rows_of(k):
        return pl.ds(k * CH, CH)

    ent_copies = [
        remote(eb.at[rows_of(k)], part.at[rep, rows_of(k)], e_s.at[k], e_r.at[k], far)
        for k in range(CHUNKS)
    ]
    for k in range(CHUNKS):
        ent_copies[k].start()

    part[:, D:PAD, :] = jnp.zeros((REP, PAD - D, ROWS), BF)
    eb[D:PAD, :] = jnp.zeros((PAD - D, ROWS), BF)
    qf[D:PAD, :] = jnp.zeros((PAD - D, EDGES), F32)
    uf[D:PAD, :] = jnp.zeros((PAD - D, EDGES), F32)
    dwf[D:PAD, :] = jnp.zeros((PAD - D, EDGES), F32)
    ids = rel_ids[...]
    owner = div5(ids)
    slot = ids - owner * REL_DEV
    owner_z = lax.shift_right_logical(owner, SHIFT_PLANE)
    owner_p = owner & (PI * CORES - 1)
    block = (owner_p & (CORES - 1)) * PI + lax.shift_right_logical(owner_p, SHIFT_CORE)
    pos = block * CB + owner_z * REL_DEV + slot
    posz = block * Z + owner_z

    ohs[...] = one_hot(iota((ROWS, EDGES), 0) == src_rows[...])
    for b in range(REP):
        ohd[b] = one_hot(iota((ROWS, EDGES), 0) + b * ROWS == dst_rows[...])

    def column(row):
        return jnp.transpose(jnp.broadcast_to(row.astype(F32), (EDGES, EDGES)))[:, :128]

    pos_col = column(pos)
    posz_col = column(posz)
    slot_col = column(slot)
    blocks = PI * CORES

    @pl.loop(0, CORES)
    def _(k):
        @pl.loop(0, PI)
        def _(n):
            at = k * PI + n
            ohx[k, pl.ds(pl.multiple_of(n * CB, 16), CB), :] = one_hot(
                iota((CB, EDGES), 0) + at * CB == pos
            )
            ohz[k, pl.ds(pl.multiple_of(n * Z, 16), Z), :] = one_hot(
                iota((Z, EDGES), 0) + at * Z == posz
            )

    lanes = iota((EDGES, 128), 1).astype(F32)
    for t in range(0, blocks * CB, 128):
        hot = one_hot(lanes + float(t) == pos_col)
        ohxt[:, t : t + 128] = hot[:, : min(128, blocks * CB - t)]
    for t in range(0, blocks * Z, 128):
        hot = one_hot(lanes + float(t) == posz_col)
        ohzt[:, t : t + 128] = hot[:, : min(128, blocks * Z - t)]
    slot_mask = lax.shift_right_logical(iota((EDGES, 128), 1), 4).astype(F32) == slot_col

    ones = jnp.ones((16, NEG_PAD), BF)
    negs[...] = jnp.full((2, NEG_PAD), -1, jnp.int32)
    negs[0:1, 0:NEG] = neg_dst[...]
    negs[1:2, 0:NEG] = neg_src[...]
    for b in range(REP):
        cnts[b] = nt(ones, one_hot(iota((ROWS, NEG_PAD), 0) + b * ROWS == negs[0:1, :]))
    cnts[REP] = nt(ones, one_hot(iota((ROWS, NEG_PAD), 0) == negs[1:2, :]))
    sf[...] = nn(eb[0:D, :], ohs[...])

    def plane_copy(n):
        return remote(g.at[c, pi], g.at[c, pi], p_s.at[n], p_r.at[n], plane_peer(n))

    def plane_arrival(n):
        came = plane_from(n)
        return remote(g.at[c, came], g.at[c, came], p_s.at[n], p_r.at[n], plane_peer(n))

    def core_copy(n):
        came = plane_from(n)
        return remote(g.at[c, came], g.at[c, came], g_s.at[n], g_r.at[n], mate)

    def core_arrival(n):
        came = plane_from(n)
        return remote(g.at[cm, came], g.at[cm, came], g_s.at[n], g_r.at[n], mate)

    @pl.loop(1, Z)
    def _(n):
        came = pl.ds(pl.multiple_of(((z + Z - n) % Z) * TILE, TILE), TILE)
        remote(zt.at[came], zt.at[came], zt_s.at[n], zt_r.at[n], device(n, 0, 0, c)).wait_recv()

    def by_kind(k):
        zz = lax.shift_right_logical(k, 4)
        s = k & 15
        kind = lax.shift_right_logical(s * 13, 6)
        return kind * CB + jnp.where(kind < 3, zz * REL_DEV + s - kind * REL_DEV, zz)

    square = (REL_ROWS, REL_ROWS)
    g[c, pi] = nn(one_hot(iota(square, 0) == by_kind(iota(square, 1))), zt[...]).astype(BF)

    @pl.loop(1, PI)
    def _(n):
        plane_copy(n).start()

    core_copy(0).start()

    y_copies = [
        remote(part.at[rep, rows_of(k)], part.at[rep, rows_of(k)], y_s.at[k], y_r.at[k], across)
        for k in range(CHUNKS)
    ]
    c1_copies = [
        remote(part.at[rep, rows_of(k)], part.at[rep, rows_of(k)], c1_s.at[k], c1_r.at[k], mate)
        for k in range(CHUNKS)
    ]
    rep_y = (1 - yh) * CORES + c
    rep_m = yh * CORES + cm
    rep_d = (1 - yh) * CORES + cm
    c2_copies = [
        remote(part.at[rep_y, rows_of(k)], part.at[rep_y, rows_of(k)], c2_s.at[k], c2_r.at[k], mate)
        for k in range(CHUNKS)
    ]

    def arrival(k, at, sends, recvs, peer):
        return remote(part.at[at, rows_of(k)], part.at[at, rows_of(k)], sends.at[k], recvs.at[k], peer)

    share = -(-(PI - 1) // CHUNKS)
    for k in range(CHUNKS):
        ent_copies[k].wait_recv()
        y_copies[k].start()
        c1_copies[k].start()

        @pl.loop(1 + k * share, min(PI, 1 + (k + 1) * share))
        def _(n):
            plane_arrival(n).wait_recv()
            core_copy(n).start()

    for k in range(CHUNKS):
        arrival(k, rep_y, y_s, y_r, across).wait_recv()
        c2_copies[k].start()

    @pl.loop(0, PI)
    def _(n):
        core_arrival(n).wait_recv()

    table = g[...].reshape(blocks, REL_ROWS, 128)
    for k in range(3):
        w = nn(ohxt[...], table[:, k * CB : (k + 1) * CB, :].reshape(blocks * CB, 128))
        wf[k * 128 : (k + 1) * 128, :] = jnp.transpose(w)
    w = nn(ohzt[...], table[:, 3 * CB :, :].reshape(blocks * Z, 128))
    fold = one_hot(
        ((iota((128, 128), 0) & 15) == iota((128, 128), 1)) & (iota((128, 128), 0) < 16 * REL_DEV)
    )
    w = nn(jnp.where(slot_mask, w, 0.0).astype(BF), fold)
    wf[384:512, :] = jnp.transpose(w)

    def parts(ref, k):
        re = pl.ds(pl.multiple_of(k * STEP, 8), STEP)
        im = pl.ds(pl.multiple_of(HALF + k * STEP, 8), STEP)
        return ref[re, :], ref[im, :]

    def put(ref, k, re_value, im_value):
        ref[pl.ds(pl.multiple_of(k * STEP, 8), STEP), :] = re_value
        ref[pl.ds(pl.multiple_of(HALF + k * STEP, 8), STEP), :] = im_value

    @pl.loop(0, STEPS)
    def _(k):
        s_re, s_im = parts(sf, k)
        w_re, w_im = parts(wf, k)
        put(qf, k, s_re * w_re - s_im * w_im, s_re * w_im + s_im * w_re)

    qb[...] = qf[0:D, :].astype(BF)
    for k in range(PAD // 128):
        at = slice(k * 128, (k + 1) * 128)
        qrow[:, at] = jnp.transpose(qf[at, :]).astype(BF)

    for k in range(CHUNKS):
        arrival(k, rep_m, c1_s, c1_r, mate).wait_recv()
        arrival(k, rep_d, c2_s, c2_r, mate).wait_recv()

    total = nn(part[0, 0:D, :], ohd[0])
    for b in range(1, REP):
        total += nn(part[b, 0:D, :], ohd[b])
    of[...] = total

    def turn(k, positive):
        w_re, w_im = parts(wf, k)
        o_re, o_im = parts(of, k)
        q_re, q_im = parts(qf, k)
        put(uf, k, w_re * o_re + w_im * o_im, w_re * o_im - w_im * o_re)
        return positive + jnp.sum(q_re * o_re + q_im * o_im, axis=0, keepdims=True)

    positive = lax.fori_loop(0, STEPS, turn, jnp.zeros((1, EDGES), F32))
    live = count[...]
    live_row = jnp.where(iota((1, EDGES), 1) < live, 1.0, 0.0)
    live_col = jnp.where(iota((EDGES, 1), 0) < live, 1.0 / NEG, 0.0)
    grad_pos = -live_row * jax.nn.sigmoid(-positive)

    for k in range(PAD // 128):
        at = slice(k * 128, (k + 1) * 128)
        urow[:, at] = jnp.transpose(uf[at, :]).astype(BF)

    def weights(scores, b):
        return (jax.nn.sigmoid(scores) * cnts[b, 0:1, :] * live_col).astype(BF)

    gs[...] = weights(nn(urow[...], eb[...]), REP)
    for b in range(REP):
        gmat[b] = weights(nn(qrow[...], part[b]), b)
    dpf[...] = nt(eb[0:D, :], gs[...])
    total = nt(part[0, 0:D, :], gmat[0])
    for b in range(1, REP):
        total += nt(part[b, 0:D, :], gmat[b])
    dqf[...] = total

    @pl.loop(0, STEPS)
    def _(k):
        s_re, s_im = parts(sf, k)
        w_re, w_im = parts(wf, k)
        o_re, o_im = parts(of, k)
        q_re, q_im = parts(qf, k)
        u_re, u_im = parts(uf, k)
        dq_re, dq_im = parts(dqf, k)
        dp_re, dp_im = parts(dpf, k)
        dq_re += grad_pos * o_re
        dq_im += grad_pos * o_im
        dp_re += grad_pos * s_re
        dp_im += grad_pos * s_im
        put(
            dof, k,
            grad_pos * q_re + w_re * dp_re - w_im * dp_im,
            grad_pos * q_im + w_re * dp_im + w_im * dp_re,
        )
        put(
            dwf, k,
            s_re * dq_re + s_im * dq_im + o_re * dp_re + o_im * dp_im,
            s_re * dq_im - s_im * dq_re + o_im * dp_re - o_re * dp_im,
        )
        put(
            dsf, k,
            w_re * dq_re + w_im * dq_im + grad_pos * u_re,
            w_re * dq_im - w_im * dq_re + grad_pos * u_im,
        )

    dob[...] = dof[...].astype(BF)

    def dc_copy(k):
        return remote(
            dest.at[cm, :, rows_of(k)], dcr.at[:, rows_of(k)], dc_s.at[k], dc_r.at[k], mate
        )

    def dy_copy(k):
        return remote(ysend.at[rows_of(k)], yrecv.at[rows_of(k)], dy_s.at[k], dy_r.at[k], across)

    def dz_copy(k):
        return remote(ezs.at[rows_of(k)], ezr.at[rows_of(k)], dz_s.at[k], dz_r.at[k], far)

    for k in range(CHUNKS):
        at = slice(k * CH, (k + 1) * CH)
        for b in range(REP):
            dest[b % CORES, b // CORES, at, :] = (
                nn(qb[at, :], gmat[b]) + nt(dob[at, :], ohd[b])
            ).astype(BF)
        dc_copy(k).start()

    for k in range(3):
        dwb[:, k * 128 : (k + 1) * 128] = jnp.transpose(dwf[k * 128 : (k + 1) * 128, :]).astype(BF)
    spread = one_hot(
        ((iota((128, 128), 1) & 15) == iota((128, 128), 0)) & (iota((128, 128), 1) < 16 * REL_DEV)
    )
    tail = nn(jnp.transpose(dwf[384:512, :]).astype(BF), spread)
    dwz[...] = jnp.where(slot_mask, tail, 0.0).astype(BF)

    def rel_blocks(core, n):
        rows = nn(ohx[core, n * GROUP * CB : (n + 1) * GROUP * CB, :], dwb[...]).astype(BF)
        ends = nn(ohz[core, n * GROUP * Z : (n + 1) * GROUP * Z, :], dwz[...]).astype(BF)
        for m in range(GROUP):
            for k in range(3):
                rblk[core, n * GROUP + m, k * CB : (k + 1) * CB, :] = rows[
                    m * CB : (m + 1) * CB, k * 128 : (k + 1) * 128
                ]
            rblk[core, n * GROUP + m, 3 * CB :, :] = ends[m * Z : (m + 1) * Z, :]

    def rc_copy(n):
        at = pl.ds(n * GROUP, GROUP)
        return remote(rblk.at[cm, at], rcr.at[at], rc_s.at[n], rc_r.at[n], mate)

    for n in range(GROUPS):
        rel_blocks(cm, n)
        rc_copy(n).start()

    for k in range(CHUNKS):
        at = slice(k * CH, (k + 1) * CH)
        dc_copy(k).wait_recv()
        ysend[at, :] = (dest[c, 1 - yh, at, :].astype(F32) + dcr[1 - yh, at, :].astype(F32)).astype(BF)
        dy_copy(k).start()

    for n in range(GROUPS):
        rel_blocks(c, n)

    for k in range(CHUNKS):
        at = slice(k * CH, (k + 1) * CH)
        dy_copy(k).wait_recv()
        ezs[at, :] = (
            dest[c, yh, at, :].astype(F32)
            + dcr[yh, at, :].astype(F32)
            + yrecv[at, :].astype(F32)
        ).astype(BF)
        dz_copy(k).start()

    for n in range(GROUPS):
        rc_copy(n).wait_recv()

    def rp_copy(n):
        return remote(rblk.at[c, plane_index(n)], rpr.at[n], rp_s.at[n], rp_r.at[n], plane_peer(n))

    def both(at):
        return rblk[c, at].astype(F32) + rcr[at].astype(F32)

    @pl.loop(1, PI)
    def _(n):
        at = plane_index(n)
        rblk[c, at] = both(at).astype(BF)
        rp_copy(n).start()

    ds_hi = dsf[...].astype(BF)
    ds_lo = (dsf[...] - ds_hi.astype(F32)).astype(BF)
    uhalf = uf[0:D, :].astype(BF)
    sf[...] = nn(uhalf, gs[...]) + nt(ds_hi, ohs[...]) + nt(ds_lo, ohs[...])

    def add_plane(n, acc):
        rp_copy(n).wait_recv()
        return acc + rpr[n].astype(F32)

    plane_sum = lax.fori_loop(1, PI, add_plane, both(pi))
    to_z = one_hot(iota(square, 1) == by_kind(iota(square, 0)))
    zsend[...] = nn(to_z, plane_sum.astype(BF)).astype(BF)

    def rz_copy(n):
        at = pl.ds(pl.multiple_of(((z + n) % Z) * TILE, TILE), TILE)
        return remote(zsend.at[at], zrecv.at[n], rz_s.at[n], rz_r.at[n], device(n, 0, 0, c))

    @pl.loop(1, Z)
    def _(n):
        rz_copy(n).start()

    for k in range(CHUNKS):
        dz_copy(k).wait_recv()
    ent_grad = sf[...] + ezr[...].astype(F32)
    fresh = state[...] + jnp.sum(ent_grad * ent_grad, axis=0, keepdims=True) * (1.0 / D)
    new_state[...] = fresh
    new_ent[...] = ent[...] - ent_grad * (0.5 / jnp.sqrt(fresh))

    def add_tile(n, acc):
        rz_copy(n).wait_recv()
        return acc + zrecv[n].astype(F32)

    tf[...] = lax.fori_loop(1, Z, add_tile, zsend[own_tile, :].astype(F32))
    own_slot = lax.shift_right_logical(lane, 4) == row5
    ends = jnp.where(own_slot, jnp.broadcast_to(tf[15:16, :], (REL_DEV, 128)), 0.0)
    fold_f = fold.astype(F32)
    ends = jnp.dot(ends, fold_f, precision=lax.Precision.HIGHEST, preferred_element_type=F32)
    pieces = [tf[k * REL_DEV : (k + 1) * REL_DEV, :] for k in range(3)] + [ends]
    squares = jnp.sum(sum(piece * piece for piece in pieces), axis=1, keepdims=True)
    eye = iota((REL_DEV, REL_DEV), 0) == iota((REL_DEV, REL_DEV), 1)
    old = jnp.broadcast_to(rel_state[...], (REL_DEV, REL_DEV))
    old = jnp.sum(jnp.where(eye, old, 0.0), axis=1, keepdims=True)
    fresh = old + squares * (1.0 / D)
    new_rel_state[...] = jnp.sum(
        jnp.where(eye, jnp.broadcast_to(fresh, (REL_DEV, REL_DEV)), 0.0), axis=0, keepdims=True
    )
    scale = 0.5 / jnp.sqrt(fresh)
    for k in range(3):
        at = slice(k * 128, (k + 1) * 128)
        new_rel[:, at] = rel[:, at] - pieces[k] * scale
    new_rel[:, 384:400] = rel[:, 384:400] - ends[:, 0:16] * scale

    for k in range(CHUNKS):
        ent_copies[k].wait_send()
        y_copies[k].wait_send()
        c1_copies[k].wait_send()
        c2_copies[k].wait_send()
        dc_copy(k).wait_send()
        dy_copy(k).wait_send()
        dz_copy(k).wait_send()
    for n in range(GROUPS):
        rc_copy(n).wait_send()
    core_copy(0).wait_send()

    @pl.loop(1, Z)
    def _(n):
        tile_copy(n).wait_send()
        rz_copy(n).wait_send()

    @pl.loop(1, PI)
    def _(n):
        plane_copy(n).wait_send()
        core_copy(n).wait_send()
        rp_copy(n).wait_send()


def scratch():
    vm = pltpu.VMEM
    dma = pltpu.SemaphoreType.DMA
    blocks = PI * CORES
    return [
        vm((PAD, ROWS), BF),
        vm((REP, PAD, ROWS), BF),
        vm((REL_ROWS, 128), BF),
        vm((CORES, PI, REL_ROWS, 128), BF),
        vm((TILE, 128), F32),
        vm((ROWS, EDGES), BF),
        vm((REP, ROWS, EDGES), BF),
        vm((CORES, PI * CB, EDGES), BF),
        vm((CORES, PI * Z, EDGES), BF),
        vm((EDGES, blocks * CB), BF),
        vm((EDGES, blocks * Z), BF),
        vm((2, NEG_PAD), jnp.int32),
        vm((REP + 1, 16, ROWS), F32),
        vm((D, EDGES), F32),
        vm((PAD, EDGES), F32),
        vm((D, EDGES), F32),
        vm((PAD, EDGES), F32),
        vm((PAD, EDGES), F32),
        vm((D, EDGES), F32),
        vm((D, EDGES), F32),
        vm((D, EDGES), F32),
        vm((D, EDGES), F32),
        vm((PAD, EDGES), F32),
        vm((D, EDGES), BF),
        vm((EDGES, PAD), BF),
        vm((EDGES, PAD), BF),
        vm((REP, EDGES, ROWS), BF),
        vm((EDGES, ROWS), BF),
        vm((D, EDGES), BF),
        vm((EDGES, 384), BF),
        vm((EDGES, 128), BF),
        vm((CORES, YH, D, ROWS), BF),
        vm((YH, D, ROWS), BF),
        vm((D, ROWS), BF),
        vm((D, ROWS), BF),
        vm((D, ROWS), BF),
        vm((D, ROWS), BF),
        vm((CORES, PI, REL_ROWS, 128), BF),
        vm((PI, REL_ROWS, 128), BF),
        vm((PI, REL_ROWS, 128), BF),
        vm((REL_ROWS, 128), BF),
        vm((Z, TILE, 128), BF),
        dma((Z,)), dma((Z,)),
        dma((CHUNKS,)), dma((CHUNKS,)),
        dma((CHUNKS,)), dma((CHUNKS,)),
        dma((CHUNKS,)), dma((CHUNKS,)),
        dma((CHUNKS,)), dma((CHUNKS,)),
        dma((PI,)), dma((PI,)),
        dma((PI,)), dma((PI,)),
        dma((CHUNKS,)), dma((CHUNKS,)),
        dma((CHUNKS,)), dma((CHUNKS,)),
        dma((CHUNKS,)), dma((CHUNKS,)),
        dma((GROUPS,)), dma((GROUPS,)),
        dma((PI,)), dma((PI,)),
        dma((Z,)), dma((Z,)),
    ]


def local(
    entities, ent_state, relations, rel_state, src_rows, dst_rows, rel_ids, neg_src, neg_dst, edge_count
):
    vmem = pl.BlockSpec(memory_space=pltpu.VMEM)
    new_ent, new_state, new_rel, new_rel_state = pl.pallas_call(
        kernel,
        out_shape=(
            jax.ShapeDtypeStruct((D, ROWS), F32),
            jax.ShapeDtypeStruct((1, ROWS), F32),
            jax.ShapeDtypeStruct((REL_DEV, D), F32),
            jax.ShapeDtypeStruct((1, REL_DEV), F32),
        ),
        in_specs=[vmem] * 10,
        out_specs=(vmem,) * 4,
        scratch_shapes=scratch(),
        compiler_params=pltpu.CompilerParams(
            collective_id=0, has_side_effects=True, vmem_limit_bytes=56 * 1024 * 1024
        ),
        name="bucket_round",
    )(
        entities.T,
        ent_state.reshape(1, ROWS),
        relations,
        rel_state.reshape(1, REL_DEV),
        src_rows,
        dst_rows,
        rel_ids,
        neg_src,
        neg_dst,
        edge_count.reshape(1, 1),
    )
    return (new_ent.T, new_state.reshape(ROWS), new_rel, new_rel_state.reshape(REL_DEV))


def solution(mesh):
    rows = P(("dom", "rep"), None)
    flat = P(("dom", "rep"))
    return jax.shard_map(
        local,
        mesh=mesh,
        in_specs=(rows, flat, rows, flat, rows, rows, rows, rows, rows, flat),
        out_specs=(rows, flat, rows, flat),
        check_vma=False,
    )
```

```python
import jax
import jax.numpy as jnp
from jax import lax
from jax.experimental import pallas as pl
from jax.experimental.pallas import tpu as pltpu
from jax.sharding import PartitionSpec as P

Z, X, YL, YH, CORES = 16, 4, 2, 2, 2
Y = YL * YH
PI = X * Y
D = 400
HALF = D // 2
PAD = 512
ROWS = 256
EDGES = 256
NEG = 1000
NEG_PAD = 1024
REP = YH * CORES
REL_DEV = 5
TILE = 16
SLOTS = Z * TILE
CB = Z * REL_DEV
NR = 2 * Z
FR = CB - NR
NEAR_Z = -(-NR // REL_DEV)
NEAR_ROWS = 3 * NR
FAR_ROWS = 3 * FR + Z
FH = FAR_ROWS // 2
HALVES = ROWS // 128
SPLIT = 208
PIECES = [(at, size, h) for h in range(HALVES) for at, size in ((0, SPLIT), (SPLIT, D - SPLIT))]
CHUNKS = len(PIECES)
PER_HALF = CHUNKS // HALVES
STEP = 40
STEPS = HALF // STEP
SHIFT_PLANE = (PI * CORES).bit_length() - 1
SHIFT_CORE = CORES.bit_length() - 1
SHIFT_YH = SHIFT_CORE + YH.bit_length() - 1
SHIFT_YL = SHIFT_YH + YL.bit_length() - 1
BF = jnp.bfloat16
F32 = jnp.float32
MESH = pl.DeviceIdType.MESH


def nn(a, b):
    return jnp.dot(a, b, preferred_element_type=F32)


def nt(a, b):
    return lax.dot_general(a, b, (((1,), (1,)), ((), ())), preferred_element_type=F32)


def iota(shape, dim):
    return lax.broadcasted_iota(jnp.int32, shape, dim)


def one_hot(cond):
    return jnp.where(cond, 1.0, 0.0).astype(BF)


def div5(v):
    return lax.shift_right_logical(v * 52429, 18)


def remote(src, dst, send, recv, peer):
    return pltpu.make_async_remote_copy(
        src_ref=src, dst_ref=dst, send_sem=send, recv_sem=recv, device_id=peer, device_id_type=MESH
    )


def kernel(
    ent, rel, src_rows, dst_rows, rel_ids, neg_src, neg_dst, count,
    ent_grad, rel_grad,
    ent_here, eb, part, zt, gn, gf, tf, ohs, ohd, ohn, ohf, ohz, ohnt, ohft, ohzt, negs, cnts,
    sf, wf, of, qf, uf, dqf, dpf, dof, dsf, dwf,
    qb, qrow, urow, gmat, gs, dob, ub, sscale, dscale, dwb, dwz,
    dest, dcr, ysend, yrecv, ezs, ezr, rn, rf, rcn, rcf, rn1, rn2, rx1, rx2, ry1, ry2, sn, sx, sy, zsend, zrecv,
    zt_s, zt_r, e_s, e_r, y_s, y_r, m_s, m_r, d_s, d_r, n1_s, n1_r, n2_s, n2_r, f1_s, f1_r, f2_s, f2_r, gn_s, gn_r, gf_s, gf_r,
    dc_s, dc_r, dy_s, dy_r, dz_s, dz_r, rcn_s, rcn_r, rcf_s, rcf_r, rn1_s, rn1_r, rn2_s, rn2_r, rx1_s, rx1_r, rx2_s, rx2_r, ry1_s, ry1_r, ry2_s, ry2_r,
    rz_s, rz_r, in_sem,
):
    dom = lax.axis_index("dom")
    rep = lax.axis_index("rep")
    z = dom // (X * YL)
    x = (dom // YL) % X
    yl = dom % YL
    yh = rep // CORES
    c = rep % CORES
    y = yh * YL + yl
    cm = 1 - c

    def device(dz, dx, dy, core):
        yy = (y + dy) % Y
        return {
            "dom": (((z + dz) % Z) * X + (x + dx) % X) * YL + yy % YL,
            "rep": (yy // YL) * CORES + core,
        }

    def x_at(n):
        return (x + X + n) % X

    def y_at(n):
        return (y + Y + n) % Y

    mate = device(0, 0, 0, cm)
    across = device(0, 0, YL, c)
    far = device(Z // 2, 0, 0, c)

    barrier = pltpu.get_barrier_semaphore()

    @pl.loop(1, Z)
    def _(n):
        pl.semaphore_signal(barrier, inc=1, device_id=device(n, 0, 0, c), device_id_type=MESH)

    for n in range(1, X):
        pl.semaphore_signal(barrier, inc=1, device_id=device(0, n, 0, c), device_id_type=MESH)
    for n in range(1, Y):
        pl.semaphore_signal(barrier, inc=1, device_id=device(0, 0, n, c), device_id_type=MESH)
    pl.semaphore_signal(barrier, inc=1, device_id=mate, device_id_type=MESH)

    read = pltpu.make_async_copy(ent, ent_here, in_sem)
    read.start()

    lane = iota((REL_DEV, 128), 1)
    row5 = iota((REL_DEV, 128), 0)
    for k in range(3):
        tf[k * REL_DEV : (k + 1) * REL_DEV, :] = rel[:, k * 128 : (k + 1) * 128]
    spread16 = one_hot((iota((16, 128), 1) & 15) == iota((16, 128), 0))
    last = nn(rel[:, 384:400].astype(BF), spread16)
    last = jnp.where(lax.shift_right_logical(lane, 4) == row5, last, 0.0)
    tf[15:16, :] = jnp.sum(last, axis=0, keepdims=True)
    zt[0:TILE, :] = tf[...].astype(BF)

    pl.semaphore_wait(barrier, (Z - 1) + (X - 1) + (Y - 1) + 1)

    def slot_device(n):
        return device(jnp.where(n % 2 == 1, (n + 1) // 2, Z - n // 2), 0, 0, c)

    def slot_there(n):
        return jnp.where(n % 2 == 1, jnp.minimum(n + 1, Z - 1), n - 1) if Z > 2 else n

    def tile_of(n):
        return pl.ds(pl.multiple_of(n * TILE, TILE), TILE)

    def tile_copy(n):
        at = slot_there(n)
        return remote(
            zt.at[tile_of(0)], zt.at[tile_of(at)], zt_s.at[n], zt_r.at[at], slot_device(n)
        )

    def tile_arrival(n):
        return remote(zt.at[tile_of(n)], zt.at[tile_of(n)], zt_s.at[n], zt_r.at[n], slot_device(n))

    @pl.loop(NEAR_Z, Z)
    def _(n):
        tile_copy(n).start()

    @pl.loop(1, NEAR_Z)
    def _(n):
        tile_copy(n).start()

    def piece(k):
        at, size, h = PIECES[k]
        return pl.ds(at, size), pl.ds(h * 128, 128)

    def slices(k):
        at, size, h = PIECES[k]
        return slice(at, at + size), slice(h * 128, (h + 1) * 128)

    ent_copies = [
        remote(eb.at[piece(k)], part.at[(rep, *piece(k))], e_s.at[k], e_r.at[k], far)
        for k in range(CHUNKS)
    ]

    read.wait()
    eb[0:D, :] = ent_here[...].astype(BF)
    part[:, D:PAD, :] = jnp.zeros((REP, PAD - D, ROWS), BF)
    eb[D:PAD, :] = jnp.zeros((PAD - D, ROWS), BF)
    qf[D:PAD, :] = jnp.zeros((PAD - D, EDGES), F32)
    uf[D:PAD, :] = jnp.zeros((PAD - D, EDGES), F32)
    dwf[D:PAD, :] = jnp.zeros((PAD - D, EDGES), F32)
    ids = rel_ids[...]
    owner = div5(ids)
    slot = ids - owner * REL_DEV
    owner_z = lax.shift_right_logical(owner, SHIFT_PLANE)
    owner_p = owner & (PI * CORES - 1)
    owner_yh = lax.shift_right_logical(owner_p, SHIFT_CORE) & (YH - 1)
    owner_yl = lax.shift_right_logical(owner_p, SHIFT_YH) & (YL - 1)
    owner_x = lax.shift_right_logical(owner_p, SHIFT_YL)
    block = (((owner_p & (CORES - 1)) * X + owner_x) * YH + owner_yh) * YL + owner_yl
    ring = (owner_z + Z - z) & (Z - 1)
    order = jnp.where(ring * 2 <= Z, jnp.maximum(2 * ring - 1, 0), 2 * (Z - ring))
    row = order * REL_DEV + slot
    pos_n = jnp.where(row < NR, block * NR + row, -1)
    pos_f = jnp.where(row < NR, -1, block * FR + row - NR)
    pos_z = block * Z + order

    ohs[...] = one_hot(iota((ROWS, EDGES), 0) == src_rows[...])
    for b in range(REP):
        ohd[b] = one_hot(iota((ROWS, EDGES), 0) + b * ROWS == dst_rows[...])

    def column(row):
        return jnp.transpose(jnp.broadcast_to(row.astype(F32), (EDGES, EDGES)))[:, :128]

    slot_col = column(slot)
    blocks = PI * CORES
    lanes = iota((EDGES, 128), 1).astype(F32)
    for count_at, at, hot, hot_t in (
        (NR, pos_n, ohn, ohnt),
        (FR, pos_f, ohf, ohft),
        (Z, pos_z, ohz, ohzt),
    ):

        @pl.loop(0, PI)
        def _(n):
            for k in range(CORES):
                hot[k, pl.ds(pl.multiple_of(n * count_at, 16), count_at), :] = one_hot(
                    iota((count_at, EDGES), 0) + (k * PI + n) * count_at == at
                )

        at_col = column(at)
        for t in range(0, blocks * count_at, 128):
            value = one_hot(lanes + float(t) == at_col)
            hot_t[:, t : t + 128] = value[:, : min(128, blocks * count_at - t)]
    slot_mask = lax.shift_right_logical(iota((EDGES, 128), 1), 4).astype(F32) == slot_col

    ones = jnp.ones((16, NEG_PAD), BF)
    negs[...] = jnp.full((2, NEG_PAD), -1, jnp.int32)
    negs[0:1, 0:NEG] = neg_dst[...]
    negs[1:2, 0:NEG] = neg_src[...]
    for b in range(REP):
        cnts[b] = nt(ones, one_hot(iota((ROWS, NEG_PAD), 0) + b * ROWS == negs[0:1, :]))
    cnts[REP] = nt(ones, one_hot(iota((ROWS, NEG_PAD), 0) == negs[1:2, :]))
    sf[...] = nn(eb[0:D, :], ohs[...])

    live = count[...]
    live_row = jnp.where(iota((1, EDGES), 1) < live, 1.0, 0.0)
    live_col = jnp.where(iota((EDGES, ROWS), 0) < live, 1.0 / NEG, 0.0)
    which = lax.shift_right_logical(dst_rows[...], 7) & (HALVES - 1)
    which_col = column(which)
    which_col = jnp.concatenate([which_col, which_col], axis=1)
    for b in range(REP):
        dscale[b] = cnts[b, 0:1, :] * live_col
    for h in range(HALVES):
        sscale[h] = jnp.where(which_col == float(h), cnts[REP, 0:1, :] * live_col, 0.0)

    for k in range(CHUNKS):
        ent_copies[k].start()

    def along_x(n):
        return device(0, n, 0, c)

    def along_y(n):
        return device(0, 0, n, c)

    def same(ref, sends, recvs, n, peer):
        return remote(ref, ref, sends.at[n], recvs.at[n], peer)

    def near_one(n, dx):
        return same(gn.at[c, x_at(dx), y], n1_s, n1_r, n, along_x(n))

    def near_line(n, dy):
        return same(gn.at[c, :, y_at(dy)], n2_s, n2_r, n, along_y(n))

    def far_one(n, dy):
        return same(gf.at[c, x, y_at(dy)], f1_s, f1_r, n, along_y(n))

    def far_line(n, dx):
        return same(gf.at[c, x_at(dx)], f2_s, f2_r, n, along_x(n))

    def near_core(n, core):
        return same(gn.at[core, :, y_at(-n)], gn_s, gn_r, n, mate)

    def far_core(n, core):
        return same(gf.at[core, x_at(-n)], gf_s, gf_r, n, mate)

    def parts_of(k):
        at = lax.shift_right_logical(k, 4)
        s = k & 15
        kind = lax.shift_right_logical(s * 13, 6)
        r = at * REL_DEV + s - kind * REL_DEV
        near = jnp.where((kind < 3) & (r < NR), kind * NR + r, -1)
        distant = jnp.where(r < NR, -1, kind * FR + r - NR)
        return near, jnp.where(kind == 3, 3 * FR + at, distant)

    @pl.loop(1, NEAR_Z)
    def _(n):
        tile_arrival(n).wait_recv()

    shape = (NEAR_ROWS, NEAR_Z * TILE)
    pick = one_hot(iota(shape, 0) == parts_of(iota(shape, 1))[0])
    gn[c, x, y] = nn(pick, zt[0 : NEAR_Z * TILE, :]).astype(BF)
    for n in range(1, X):
        near_one(n, 0).start()

    @pl.loop(NEAR_Z, Z)
    def _(n):
        tile_arrival(n).wait_recv()

    shape = (FAR_ROWS, SLOTS)
    pick = one_hot(iota(shape, 0) == parts_of(iota(shape, 1))[1])
    gf[c, x, y] = nn(pick, zt[...]).astype(BF)
    for n in range(1, Y):
        far_one(n, 0).start()
    for n in range(1, X):
        near_one(n, -n).wait_recv()
    for n in range(1, Y):
        near_line(n, 0).start()
    near_core(0, c).start()
    for n in range(1, Y):
        far_one(n, -n).wait_recv()
    for n in range(1, X):
        far_line(n, 0).start()
    far_core(0, c).start()
    for n in range(1, Y):
        near_line(n, -n).wait_recv()
        near_core(n, c).start()

    at_y = (1 - yh) * CORES + c
    at_mate = yh * CORES + cm
    at_both = (1 - yh) * CORES + cm

    def entity_copy(k, at, sends, recvs, peer):
        ref = part.at[(at, *piece(k))]
        return remote(ref, ref, sends.at[k], recvs.at[k], peer)

    def entity_on(k):
        ent_copies[k].wait_recv()
        entity_copy(k, rep, y_s, y_r, across).start()
        entity_copy(k, rep, m_s, m_r, mate).start()

    def entity_over(k):
        entity_copy(k, at_y, y_s, y_r, across).wait_recv()
        entity_copy(k, at_y, d_s, d_r, mate).start()

    entity_on(0)
    entity_on(1)
    entity_over(0)
    for n in range(1, X):
        far_line(n, -n).wait_recv()
        far_core(n, c).start()
    entity_over(1)
    for n in range(Y):
        near_core(n, cm).wait_recv()
    for n in range(X):
        far_core(n, cm).wait_recv()

    near_table = gn[...].reshape(blocks, NEAR_ROWS, 128)
    far_table = gf[...].reshape(blocks, FAR_ROWS, 128)
    for k in range(3):
        w = nn(ohnt[...], near_table[:, k * NR : (k + 1) * NR, :].reshape(blocks * NR, 128))
        w += nn(ohft[...], far_table[:, k * FR : (k + 1) * FR, :].reshape(blocks * FR, 128))
        wf[k * 128 : (k + 1) * 128, :] = jnp.transpose(w)
    w = nn(ohzt[...], far_table[:, 3 * FR :, :].reshape(blocks * Z, 128))
    fold = one_hot(
        ((iota((128, 128), 0) & 15) == iota((128, 128), 1)) & (iota((128, 128), 0) < 16 * REL_DEV)
    )
    w = nn(jnp.where(slot_mask, w, 0.0).astype(BF), fold)
    wf[384:512, :] = jnp.transpose(w)

    def parts(ref, k):
        re = pl.ds(pl.multiple_of(k * STEP, 8), STEP)
        im = pl.ds(pl.multiple_of(HALF + k * STEP, 8), STEP)
        return ref[re, :], ref[im, :]

    def put(ref, k, re_value, im_value):
        ref[pl.ds(pl.multiple_of(k * STEP, 8), STEP), :] = re_value
        ref[pl.ds(pl.multiple_of(HALF + k * STEP, 8), STEP), :] = im_value

    @pl.loop(0, STEPS)
    def _(k):
        s_re, s_im = parts(sf, k)
        w_re, w_im = parts(wf, k)
        put(qf, k, s_re * w_re - s_im * w_im, s_re * w_im + s_im * w_re)

    qb[...] = qf[0:D, :].astype(BF)
    for k in range(PAD // 128):
        at = slice(k * 128, (k + 1) * 128)
        qrow[:, at] = jnp.transpose(qf[at, :]).astype(BF)

    def half(h):
        lanes = slice(h * 128, (h + 1) * 128)
        for k in range(h * PER_HALF, (h + 1) * PER_HALF):
            entity_copy(k, at_mate, m_s, m_r, mate).wait_recv()
            entity_copy(k, at_both, d_s, d_r, mate).wait_recv()
        total = nn(part[0, 0:D, lanes], ohd[0, lanes, :])
        for b in range(1, REP):
            total += nn(part[b, 0:D, lanes], ohd[b, lanes, :])
        of[...] = total

        def turn(k, positive):
            w_re, w_im = parts(wf, k)
            o_re, o_im = parts(of, k)
            q_re, q_im = parts(qf, k)
            put(uf, k, w_re * o_re + w_im * o_im, w_re * o_im - w_im * o_re)
            return positive + jnp.sum(q_re * o_re + q_im * o_im, axis=0, keepdims=True)

        positive = lax.fori_loop(0, STEPS, turn, jnp.zeros((1, EDGES), F32))
        grad_pos = jnp.where(which == h, -live_row * jax.nn.sigmoid(-positive), 0.0)
        ub[h] = uf[0:D, :].astype(BF)
        for k in range(PAD // 128):
            at = slice(k * 128, (k + 1) * 128)
            urow[:, at] = jnp.transpose(uf[at, :]).astype(BF)
        gs[h] = (jax.nn.sigmoid(nn(urow[...], eb[...])) * sscale[h]).astype(BF)
        for b in range(REP):
            scores = nn(qrow[...], part[b, :, lanes])
            gmat[b, :, lanes] = (jax.nn.sigmoid(scores) * dscale[b, :, lanes]).astype(BF)
        dpf[...] = nt(eb[0:D, :], gs[h])
        total = nt(part[0, 0:D, lanes], gmat[0, :, lanes])
        for b in range(1, REP):
            total += nt(part[b, 0:D, lanes], gmat[b, :, lanes])
        dqf[...] = total

        @pl.loop(0, STEPS)
        def _(k):
            s_re, s_im = parts(sf, k)
            w_re, w_im = parts(wf, k)
            o_re, o_im = parts(of, k)
            q_re, q_im = parts(qf, k)
            u_re, u_im = parts(uf, k)
            dq_re, dq_im = parts(dqf, k)
            dp_re, dp_im = parts(dpf, k)
            dq_re += grad_pos * o_re
            dq_im += grad_pos * o_im
            dp_re += grad_pos * s_re
            dp_im += grad_pos * s_im
            put(
                dof, k,
                grad_pos * q_re + w_re * dp_re - w_im * dp_im,
                grad_pos * q_im + w_re * dp_im + w_im * dp_re,
            )
            dw_re = s_re * dq_re + s_im * dq_im + o_re * dp_re + o_im * dp_im
            dw_im = s_re * dq_im - s_im * dq_re + o_im * dp_re - o_re * dp_im
            ds_re = w_re * dq_re + w_im * dq_im + grad_pos * u_re
            ds_im = w_re * dq_im - w_im * dq_re + grad_pos * u_im
            if h:
                before_re, before_im = parts(dwf, k)
                dw_re += before_re
                dw_im += before_im
                before_re, before_im = parts(dsf, k)
                ds_re += before_re
                ds_im += before_im
            put(dwf, k, dw_re, dw_im)
            put(dsf, k, ds_re, ds_im)

        dob[h] = dof[...].astype(BF)

    def dc_copy(k):
        f, rows = piece(k)
        return remote(dest.at[cm, :, f, rows], dcr.at[:, f, rows], dc_s.at[k], dc_r.at[k], mate)

    def dy_copy(k):
        return remote(ysend.at[piece(k)], yrecv.at[piece(k)], dy_s.at[k], dy_r.at[k], across)

    def dz_copy(k):
        return remote(ezs.at[piece(k)], ezr.at[piece(k)], dz_s.at[k], dz_r.at[k], far)

    def dest_chunk(k):
        f, rows = slices(k)
        h = PIECES[k][2]
        for b in range(REP):
            dest[b % CORES, b // CORES, f, rows] = (
                nn(qb[f, :], gmat[b, :, rows]) + nt(dob[h, f, :], ohd[b, rows, :])
            ).astype(BF)
        dc_copy(k).start()

    def dest_across(k):
        f, rows = slices(k)
        dc_copy(k).wait_recv()
        mine = dest[c, 1 - yh, f, rows].astype(F32) + dcr[1 - yh, f, rows].astype(F32)
        ysend[f, rows] = mine.astype(BF)
        dy_copy(k).start()

    def dest_home(k):
        f, rows = slices(k)
        mine = dest[c, yh, f, rows].astype(F32) + dcr[yh, f, rows].astype(F32)
        dy_copy(k).wait_recv()
        ezs[f, rows] = (mine + yrecv[f, rows].astype(F32)).astype(BF)
        dz_copy(k).start()

    def rel_far(core, n):
        rows = nn(ohf[core, n * Y * FR : (n + 1) * Y * FR, :], dwb[...]).astype(BF)
        ends = nn(ohz[core, n * Y * Z : (n + 1) * Y * Z, :], dwz[...]).astype(BF)
        for m in range(Y):
            for k in range(3):
                rf[core, n, m, k * FR : (k + 1) * FR, :] = rows[
                    m * FR : (m + 1) * FR, k * 128 : (k + 1) * 128
                ]
            rf[core, n, m, 3 * FR :, :] = ends[m * Z : (m + 1) * Z, :]

    def rel_near(core, n):
        rows = nn(ohn[core, n * Y * NR : (n + 1) * Y * NR, :], dwb[...]).astype(BF)
        for m in range(Y):
            for k in range(3):
                rn[core, n, m, k * NR : (k + 1) * NR, :] = rows[
                    m * NR : (m + 1) * NR, k * 128 : (k + 1) * 128
                ]

    def rc_near(n):
        return remote(rn.at[cm, n], rcn.at[n], rcn_s.at[n], rcn_r.at[n], mate)

    def rc_far(n):
        return remote(rf.at[cm, n], rcf.at[n], rcf_s.at[n], rcf_r.at[n], mate)

    def x_first(n):
        ref = rf.at[c, x_at(n), :, 0:FH]
        return remote(ref, rx1.at[n], rx1_s.at[n], rx1_r.at[n], along_x(n))

    def x_second(n):
        return remote(sx.at[y_at(n)], rx2.at[n], rx2_s.at[n], rx2_r.at[n], along_y(n))

    def y_first(n):
        ref = rf.at[c, :, y_at(n), FH:FAR_ROWS]
        return remote(ref, ry1.at[n], ry1_s.at[n], ry1_r.at[n], along_y(n))

    def y_second(n):
        return remote(sy.at[x_at(n)], ry2.at[n], ry2_s.at[n], ry2_r.at[n], along_x(n))

    def near_first(n):
        return remote(rn.at[c, :, y_at(n)], rn1.at[n], rn1_s.at[n], rn1_r.at[n], along_y(n))

    def near_second(n):
        return remote(sn.at[x_at(n)], rn2.at[n], rn2_s.at[n], rn2_r.at[n], along_x(n))

    def far_to_plane():
        for n in range(X):
            rc_far(n).wait_recv()
        for n in [*range(1, X), 0]:
            at = x_at(n)
            rf[c, at] = (rf[c, at].astype(F32) + rcf[at].astype(F32)).astype(BF)
            if n:
                x_first(n).start()
        for n in range(1, Y):
            y_first(n).start()

    def near_to_y():
        for n in range(X):
            rc_near(n).wait_recv()
        for n in [*range(1, Y), 0]:
            at = y_at(n)
            rn[c, :, at] = (rn[c, :, at].astype(F32) + rcn[:, at].astype(F32)).astype(BF)
            if n:
                near_first(n).start()

    def far_turn():
        for n in range(1, X):
            x_first(n).wait_recv()
        for n in [*range(1, Y), 0]:
            at = y_at(n)
            total = rf[c, x, at, 0:FH, :].astype(F32)
            for m in range(1, X):
                total += rx1[m, at].astype(F32)
            sx[at] = total.astype(BF)
            if n:
                x_second(n).start()
        for n in range(1, Y):
            y_first(n).wait_recv()
        for n in [*range(1, X), 0]:
            at = x_at(n)
            total = rf[c, at, y, FH:FAR_ROWS, :].astype(F32)
            for m in range(1, Y):
                total += ry1[m, at].astype(F32)
            sy[at] = total.astype(BF)
            if n:
                y_second(n).start()

    def near_to_x():
        for n in range(1, Y):
            near_first(n).wait_recv()
        for n in [*range(1, X), 0]:
            at = x_at(n)
            total = rn[c, at, y].astype(F32)
            for m in range(1, Y):
                total += rn1[m, at].astype(F32)
            sn[at] = total.astype(BF)
            if n:
                near_second(n).start()

    def rz_copy(n):
        at = slot_there(n)
        return remote(zsend.at[tile_of(n)], zrecv.at[at], rz_s.at[n], rz_r.at[at], slot_device(n))

    def rz_arrival(n):
        return remote(zsend.at[tile_of(n)], zrecv.at[n], rz_s.at[n], rz_r.at[n], slot_device(n))

    half(0)
    dest_chunk(0)
    dest_chunk(1)
    entity_on(2)
    dest_across(0)
    dest_across(1)
    entity_on(3)
    entity_over(2)
    dest_home(0)
    dest_home(1)
    entity_over(3)
    half(1)
    for k in range(3):
        dwb[:, k * 128 : (k + 1) * 128] = jnp.transpose(dwf[k * 128 : (k + 1) * 128, :]).astype(BF)
    spread = one_hot(
        ((iota((128, 128), 1) & 15) == iota((128, 128), 0)) & (iota((128, 128), 1) < 16 * REL_DEV)
    )
    tail = nn(jnp.transpose(dwf[384:512, :]).astype(BF), spread)
    dwz[...] = jnp.where(slot_mask, tail, 0.0).astype(BF)
    for n in range(X):
        rel_far(cm, n)
        rc_far(n).start()
    dest_chunk(2)
    dest_chunk(3)
    for n in range(X):
        rel_near(cm, n)
        rc_near(n).start()
    for n in range(X):
        rel_far(c, n)
    far_to_plane()
    dest_across(2)
    dest_across(3)
    for n in range(X):
        rel_near(c, n)
    near_to_y()
    dest_home(2)
    dest_home(3)
    far_turn()
    near_to_x()

    ds_hi = dsf[...].astype(BF)
    ds_lo = (dsf[...] - ds_hi.astype(F32)).astype(BF)
    total = nt(ds_hi, ohs[...]) + nt(ds_lo, ohs[...])
    for h in range(HALVES):
        total += nn(ub[h], gs[h])
    sf[...] = total

    total = sx[y].astype(F32)
    for n in range(1, Y):
        x_second(n).wait_recv()
        total += rx2[n].astype(F32)
    other = sy[x].astype(F32)
    for n in range(1, X):
        y_second(n).wait_recv()
        other += ry2[n].astype(F32)
    far_sum = jnp.concatenate([total, other], axis=0).astype(BF)
    shape = (SLOTS, FAR_ROWS)
    pick = one_hot(iota(shape, 1) == parts_of(iota(shape, 0))[1])
    tiles = nn(pick, far_sum)
    zsend[NEAR_Z * TILE :, :] = tiles[NEAR_Z * TILE :, :].astype(BF)

    @pl.loop(NEAR_Z, Z)
    def _(n):
        rz_copy(n).start()

    total = sn[x].astype(F32)
    for n in range(1, X):
        near_second(n).wait_recv()
        total += rn2[n].astype(F32)
    near_sum = total.astype(BF)
    shape = (NEAR_Z * TILE, NEAR_ROWS)
    pick = one_hot(iota(shape, 1) == parts_of(iota(shape, 0))[0])
    zsend[0 : NEAR_Z * TILE, :] = (nn(pick, near_sum) + tiles[0 : NEAR_Z * TILE, :]).astype(BF)

    @pl.loop(1, NEAR_Z)
    def _(n):
        rz_copy(n).start()

    for k in range(CHUNKS):
        dz_copy(k).wait_recv()
    ent_grad[...] = sf[...] + ezr[...].astype(F32)

    def add_tile(n, acc):
        rz_arrival(n).wait_recv()
        return acc + zrecv[n].astype(F32)

    rel_grad[...] = lax.fori_loop(1, Z, add_tile, zsend[0:TILE, :].astype(F32))

    for k in range(CHUNKS):
        ent_copies[k].wait_send()
        entity_copy(k, rep, y_s, y_r, across).wait_send()
        entity_copy(k, rep, m_s, m_r, mate).wait_send()
        entity_copy(k, at_y, d_s, d_r, mate).wait_send()
        dc_copy(k).wait_send()
        dy_copy(k).wait_send()
        dz_copy(k).wait_send()
    for n in range(X):
        rc_near(n).wait_send()
        rc_far(n).wait_send()
        far_core(n, c).wait_send()
    for n in range(Y):
        near_core(n, c).wait_send()
    for n in range(1, X):
        near_one(n, 0).wait_send()
        far_line(n, 0).wait_send()
        x_first(n).wait_send()
        y_second(n).wait_send()
        near_second(n).wait_send()
    for n in range(1, Y):
        near_line(n, 0).wait_send()
        far_one(n, 0).wait_send()
        x_second(n).wait_send()
        y_first(n).wait_send()
        near_first(n).wait_send()

    @pl.loop(1, Z)
    def _(n):
        tile_copy(n).wait_send()
        rz_copy(n).wait_send()


def update(
    ent, state, rel, rel_state, ent_grad, rel_grad, new_ent, new_state, new_rel, new_rel_state
):
    grad = ent_grad[...]
    fresh = state[...] + jnp.sum(grad * grad, axis=0, keepdims=True) * (1.0 / D)
    new_state[...] = fresh
    new_ent[...] = ent[...] - grad * (0.5 / jnp.sqrt(fresh))

    lane = iota((REL_DEV, 128), 1)
    row5 = iota((REL_DEV, 128), 0)
    own_slot = lax.shift_right_logical(lane, 4) == row5
    ends = jnp.where(own_slot, jnp.broadcast_to(rel_grad[15:16, :], (REL_DEV, 128)), 0.0)
    fold_f = jnp.where(
        ((iota((128, 128), 0) & 15) == iota((128, 128), 1)) & (iota((128, 128), 0) < 16 * REL_DEV),
        1.0,
        0.0,
    )
    ends = jnp.dot(ends, fold_f, precision=lax.Precision.HIGHEST, preferred_element_type=F32)
    pieces = [rel_grad[k * REL_DEV : (k + 1) * REL_DEV, :] for k in range(3)] + [ends]
    squares = jnp.sum(sum(piece * piece for piece in pieces), axis=1, keepdims=True)
    eye = iota((REL_DEV, REL_DEV), 0) == iota((REL_DEV, REL_DEV), 1)
    old = jnp.broadcast_to(rel_state[...], (REL_DEV, REL_DEV))
    old = jnp.sum(jnp.where(eye, old, 0.0), axis=1, keepdims=True)
    fresh = old + squares * (1.0 / D)
    new_rel_state[...] = jnp.sum(
        jnp.where(eye, jnp.broadcast_to(fresh, (REL_DEV, REL_DEV)), 0.0), axis=0, keepdims=True
    )
    scale = 0.5 / jnp.sqrt(fresh)
    for k in range(3):
        at = slice(k * 128, (k + 1) * 128)
        new_rel[:, at] = rel[:, at] - pieces[k] * scale
    new_rel[:, 384:400] = rel[:, 384:400] - ends[:, 0:16] * scale


def scratch():
    vm = pltpu.VMEM
    dma = pltpu.SemaphoreType.DMA
    blocks = PI * CORES
    return [
        vm((D, ROWS), F32),
        vm((PAD, ROWS), BF),
        vm((REP, PAD, ROWS), BF),
        vm((SLOTS, 128), BF),
        vm((CORES, X, Y, NEAR_ROWS, 128), BF),
        vm((CORES, X, Y, FAR_ROWS, 128), BF),
        vm((TILE, 128), F32),
        vm((ROWS, EDGES), BF),
        vm((REP, ROWS, EDGES), BF),
        vm((CORES, PI * NR, EDGES), BF),
        vm((CORES, PI * FR, EDGES), BF),
        vm((CORES, PI * Z, EDGES), BF),
        vm((EDGES, blocks * NR), BF),
        vm((EDGES, blocks * FR), BF),
        vm((EDGES, blocks * Z), BF),
        vm((2, NEG_PAD), jnp.int32),
        vm((REP + 1, 16, ROWS), F32),
        vm((D, EDGES), F32),
        vm((PAD, EDGES), F32),
        vm((D, EDGES), F32),
        vm((PAD, EDGES), F32),
        vm((PAD, EDGES), F32),
        vm((D, EDGES), F32),
        vm((D, EDGES), F32),
        vm((D, EDGES), F32),
        vm((D, EDGES), F32),
        vm((PAD, EDGES), F32),
        vm((D, EDGES), BF),
        vm((EDGES, PAD), BF),
        vm((EDGES, PAD), BF),
        vm((REP, EDGES, ROWS), BF),
        vm((HALVES, EDGES, ROWS), BF),
        vm((HALVES, D, EDGES), BF),
        vm((HALVES, D, EDGES), BF),
        vm((HALVES, EDGES, ROWS), F32),
        vm((REP, EDGES, ROWS), F32),
        vm((EDGES, 384), BF),
        vm((EDGES, 128), BF),
        vm((CORES, YH, D, ROWS), BF),
        vm((YH, D, ROWS), BF),
        vm((D, ROWS), BF),
        vm((D, ROWS), BF),
        vm((D, ROWS), BF),
        vm((D, ROWS), BF),
        vm((CORES, X, Y, NEAR_ROWS, 128), BF),
        vm((CORES, X, Y, FAR_ROWS, 128), BF),
        vm((X, Y, NEAR_ROWS, 128), BF),
        vm((X, Y, FAR_ROWS, 128), BF),
        vm((Y, X, NEAR_ROWS, 128), BF),
        vm((X, NEAR_ROWS, 128), BF),
        vm((X, Y, FH, 128), BF),
        vm((Y, FH, 128), BF),
        vm((Y, X, FH, 128), BF),
        vm((X, FH, 128), BF),
        vm((X, NEAR_ROWS, 128), BF),
        vm((Y, FH, 128), BF),
        vm((X, FH, 128), BF),
        vm((SLOTS, 128), BF),
        vm((Z, TILE, 128), BF),
    ] + [
        dma((n,))
        for n in [Z] * 2 + [CHUNKS] * 8 + [max(X, Y)] * 12 + [CHUNKS] * 6 + [max(X, Y)] * 16 + [Z] * 2
    ] + [dma]


def local(
    entities, ent_state, relations, rel_state, src_rows, dst_rows, rel_ids, neg_src, neg_dst, edge_count
):
    vmem = pl.BlockSpec(memory_space=pltpu.VMEM)
    ent = entities.T
    ent_grad, rel_grad = pl.pallas_call(
        kernel,
        out_shape=(
            jax.ShapeDtypeStruct((D, ROWS), F32),
            jax.ShapeDtypeStruct((TILE, 128), F32),
        ),
        in_specs=[pl.BlockSpec(memory_space=pl.ANY)] + [vmem] * 7,
        out_specs=(vmem,) * 2,
        scratch_shapes=scratch(),
        compiler_params=pltpu.CompilerParams(
            collective_id=0, has_side_effects=True, vmem_limit_bytes=56 * 1024 * 1024
        ),
        name="bucket_round",
    )(
        ent, relations, src_rows, dst_rows, rel_ids, neg_src, neg_dst, edge_count.reshape(1, 1)
    )
    new_ent, new_state, new_rel, new_rel_state = pl.pallas_call(
        update,
        out_shape=(
            jax.ShapeDtypeStruct((D, ROWS), F32),
            jax.ShapeDtypeStruct((1, ROWS), F32),
            jax.ShapeDtypeStruct((REL_DEV, D), F32),
            jax.ShapeDtypeStruct((1, REL_DEV), F32),
        ),
        in_specs=[vmem] * 6,
        out_specs=(vmem,) * 4,
        name="row_update",
    )(
        ent,
        ent_state.reshape(1, ROWS),
        relations,
        rel_state.reshape(1, REL_DEV),
        ent_grad,
        rel_grad,
    )
    return (new_ent.T, new_state.reshape(ROWS), new_rel, new_rel_state.reshape(REL_DEV))


def solution(mesh):
    rows = P(("dom", "rep"), None)
    flat = P(("dom", "rep"))
    return jax.shard_map(
        local,
        mesh=mesh,
        in_specs=(rows, flat, rows, flat, rows, rows, rows, rows, rows, flat),
        out_specs=(rows, flat, rows, flat),
        check_vma=False,
    )
```

```python
import jax
import jax.numpy as jnp
from jax import lax
from jax.experimental import pallas as pl
from jax.experimental.pallas import tpu as pltpu
from jax.sharding import PartitionSpec as P

Z, X, YL, YH, CORES = 16, 4, 2, 2, 2
Y = YL * YH
PI = X * Y
D = 400
HALF = D // 2
PAD = 512
ROWS = 256
EDGES = 256
NEG = 1000
NEG_PAD = 1024
REP = YH * CORES
REL_DEV = 5
TILE = 16
SLOTS = Z * TILE
CB = Z * REL_DEV
NR = 2 * Z
FR = CB - NR
NEAR_Z = -(-NR // REL_DEV)
NEAR_ROWS = 3 * NR
FAR_ROWS = 3 * FR + Z
FH = FAR_ROWS // 2
HALVES = ROWS // 128
SPLIT = 208
PIECES = [(at, size, h) for h in range(HALVES) for at, size in ((0, SPLIT), (SPLIT, D - SPLIT))]
CHUNKS = len(PIECES)
PER_HALF = CHUNKS // HALVES
STEP = 40
STEPS = HALF // STEP
SHIFT_PLANE = (PI * CORES).bit_length() - 1
SHIFT_CORE = CORES.bit_length() - 1
SHIFT_YH = SHIFT_CORE + YH.bit_length() - 1
SHIFT_YL = SHIFT_YH + YL.bit_length() - 1
BF = jnp.bfloat16
F32 = jnp.float32
MESH = pl.DeviceIdType.MESH


def nn(a, b):
    return jnp.dot(a, b, preferred_element_type=F32)


def nt(a, b):
    return lax.dot_general(a, b, (((1,), (1,)), ((), ())), preferred_element_type=F32)


def iota(shape, dim):
    return lax.broadcasted_iota(jnp.int32, shape, dim)


def one_hot(cond):
    return jnp.where(cond, 1.0, 0.0).astype(BF)


def div5(v):
    return lax.shift_right_logical(v * 52429, 18)


def remote(src, dst, send, recv, peer):
    return pltpu.make_async_remote_copy(
        src_ref=src, dst_ref=dst, send_sem=send, recv_sem=recv, device_id=peer, device_id_type=MESH
    )


def kernel(
    ent, rel_in, src_in, dst_in, ids_in, neg_src_in, neg_dst_in, count,
    ent_grad, rel_grad,
    ent_here, rel, src_rows, dst_rows, rel_ids, neg_src, neg_dst, eb, part, zt, gn, gf, tf, ohs, ohd, ohn, ohf, ohz, ohnt, ohft, ohzt, negs, cnts,
    sf, wf, of, qf, uf, dqf, dpf, dof, dsf, dwf,
    qb, qrow, urow, gmat, gs, dob, ub, sscale, dscale, dwb, dwz,
    dest, dcr, ysend, yrecv, ezs, ezr, rn, rf, rcn, rcf, rn1, rn2, rx1, rx2, ry1, ry2, sn, sx, sy, zsend, zrecv,
    zt_s, zt_r, e_s, e_r, y_s, y_r, m_s, m_r, d_s, d_r, n1_s, n1_r, n2_s, n2_r, f1_s, f1_r, f2_s, f2_r, gn_s, gn_r, gf_s, gf_r,
    dc_s, dc_r, dy_s, dy_r, dz_s, dz_r, rcn_s, rcn_r, rcf_s, rcf_r, rn1_s, rn1_r, rn2_s, rn2_r, rx1_s, rx1_r, rx2_s, rx2_r, ry1_s, ry1_r, ry2_s, ry2_r,
    rz_s, rz_r, in_sem,
):
    dom = lax.axis_index("dom")
    rep = lax.axis_index("rep")
    z = dom // (X * YL)
    x = (dom // YL) % X
    yl = dom % YL
    yh = rep // CORES
    c = rep % CORES
    y = yh * YL + yl
    cm = 1 - c

    def device(dz, dx, dy, core):
        yy = (y + dy) % Y
        return {
            "dom": (((z + dz) % Z) * X + (x + dx) % X) * YL + yy % YL,
            "rep": (yy // YL) * CORES + core,
        }

    def x_at(n):
        return (x + X + n) % X

    def y_at(n):
        return (y + Y + n) % Y

    mate = device(0, 0, 0, cm)
    across = device(0, 0, YL, c)
    far = device(Z // 2, 0, 0, c)

    reads = [
        pltpu.make_async_copy(source, here, in_sem.at[n])
        for n, (source, here) in enumerate(
            (
                (rel_in, rel),
                (ent, ent_here),
                (src_in, src_rows),
                (dst_in, dst_rows),
                (ids_in, rel_ids),
                (neg_src_in, neg_src),
                (neg_dst_in, neg_dst),
            )
        )
    ]

    barrier = pltpu.get_barrier_semaphore()

    @pl.loop(1, Z)
    def _(n):
        pl.semaphore_signal(barrier, inc=1, device_id=device(n, 0, 0, c), device_id_type=MESH)

    for n in range(1, X):
        pl.semaphore_signal(barrier, inc=1, device_id=device(0, n, 0, c), device_id_type=MESH)
    for n in range(1, Y):
        pl.semaphore_signal(barrier, inc=1, device_id=device(0, 0, n, c), device_id_type=MESH)
    pl.semaphore_signal(barrier, inc=1, device_id=mate, device_id_type=MESH)

    for read in reads:
        read.start()

    reads[0].wait()
    lane = iota((REL_DEV, 128), 1)
    row5 = iota((REL_DEV, 128), 0)
    for k in range(3):
        tf[k * REL_DEV : (k + 1) * REL_DEV, :] = rel[:, k * 128 : (k + 1) * 128]
    spread16 = one_hot((iota((16, 128), 1) & 15) == iota((16, 128), 0))
    last = nn(rel[:, 384:400].astype(BF), spread16)
    last = jnp.where(lax.shift_right_logical(lane, 4) == row5, last, 0.0)
    tf[15:16, :] = jnp.sum(last, axis=0, keepdims=True)
    zt[0:TILE, :] = tf[...].astype(BF)

    pl.semaphore_wait(barrier, (Z - 1) + (X - 1) + (Y - 1) + 1)

    def slot_device(n):
        return device(jnp.where(n % 2 == 1, (n + 1) // 2, Z - n // 2), 0, 0, c)

    def slot_there(n):
        return jnp.where(n % 2 == 1, jnp.minimum(n + 1, Z - 1), n - 1) if Z > 2 else n

    def tile_of(n):
        return pl.ds(pl.multiple_of(n * TILE, TILE), TILE)

    def tile_copy(n):
        at = slot_there(n)
        return remote(
            zt.at[tile_of(0)], zt.at[tile_of(at)], zt_s.at[n], zt_r.at[at], slot_device(n)
        )

    def tile_arrival(n):
        return remote(zt.at[tile_of(n)], zt.at[tile_of(n)], zt_s.at[n], zt_r.at[n], slot_device(n))

    @pl.loop(NEAR_Z, Z)
    def _(n):
        tile_copy(n).start()

    @pl.loop(1, NEAR_Z)
    def _(n):
        tile_copy(n).start()

    def piece(k):
        at, size, h = PIECES[k]
        return pl.ds(at, size), pl.ds(h * 128, 128)

    def slices(k):
        at, size, h = PIECES[k]
        return slice(at, at + size), slice(h * 128, (h + 1) * 128)

    ent_copies = [
        remote(eb.at[piece(k)], part.at[(rep, *piece(k))], e_s.at[k], e_r.at[k], far)
        for k in range(CHUNKS)
    ]

    for read in reads[1:]:
        read.wait()
    eb[0:D, :] = ent_here[...].astype(BF)
    part[:, D:PAD, :] = jnp.zeros((REP, PAD - D, ROWS), BF)
    eb[D:PAD, :] = jnp.zeros((PAD - D, ROWS), BF)
    qf[D:PAD, :] = jnp.zeros((PAD - D, EDGES), F32)
    uf[D:PAD, :] = jnp.zeros((PAD - D, EDGES), F32)
    dwf[D:PAD, :] = jnp.zeros((PAD - D, EDGES), F32)
    ids = rel_ids[...]
    owner = div5(ids)
    slot = ids - owner * REL_DEV
    owner_z = lax.shift_right_logical(owner, SHIFT_PLANE)
    owner_p = owner & (PI * CORES - 1)
    owner_yh = lax.shift_right_logical(owner_p, SHIFT_CORE) & (YH - 1)
    owner_yl = lax.shift_right_logical(owner_p, SHIFT_YH) & (YL - 1)
    owner_x = lax.shift_right_logical(owner_p, SHIFT_YL)
    block = (((owner_p & (CORES - 1)) * X + owner_x) * YH + owner_yh) * YL + owner_yl
    ring = (owner_z + Z - z) & (Z - 1)
    order = jnp.where(ring * 2 <= Z, jnp.maximum(2 * ring - 1, 0), 2 * (Z - ring))
    row = order * REL_DEV + slot
    pos_n = jnp.where(row < NR, block * NR + row, -1)
    pos_f = jnp.where(row < NR, -1, block * FR + row - NR)
    pos_z = block * Z + order

    ohs[...] = one_hot(iota((ROWS, EDGES), 0) == src_rows[...])
    for b in range(REP):
        ohd[b] = one_hot(iota((ROWS, EDGES), 0) + b * ROWS == dst_rows[...])

    def column(row):
        return jnp.transpose(jnp.broadcast_to(row.astype(F32), (EDGES, EDGES)))[:, :128]

    slot_col = column(slot)
    blocks = PI * CORES
    lanes = iota((EDGES, 128), 1).astype(F32)
    for count_at, at, hot, hot_t in (
        (NR, pos_n, ohn, ohnt),
        (FR, pos_f, ohf, ohft),
        (Z, pos_z, ohz, ohzt),
    ):

        @pl.loop(0, PI)
        def _(n):
            for k in range(CORES):
                hot[k, pl.ds(pl.multiple_of(n * count_at, 16), count_at), :] = one_hot(
                    iota((count_at, EDGES), 0) + (k * PI + n) * count_at == at
                )

        at_col = column(at)
        for t in range(0, blocks * count_at, 128):
            value = one_hot(lanes + float(t) == at_col)
            hot_t[:, t : t + 128] = value[:, : min(128, blocks * count_at - t)]
    slot_mask = lax.shift_right_logical(iota((EDGES, 128), 1), 4).astype(F32) == slot_col

    ones = jnp.ones((16, NEG_PAD), BF)
    negs[...] = jnp.full((2, NEG_PAD), -1, jnp.int32)
    negs[0:1, 0:NEG] = neg_dst[...]
    negs[1:2, 0:NEG] = neg_src[...]
    for b in range(REP):
        cnts[b] = nt(ones, one_hot(iota((ROWS, NEG_PAD), 0) + b * ROWS == negs[0:1, :]))
    cnts[REP] = nt(ones, one_hot(iota((ROWS, NEG_PAD), 0) == negs[1:2, :]))
    sf[...] = nn(eb[0:D, :], ohs[...])

    live = count[...]
    live_row = jnp.where(iota((1, EDGES), 1) < live, 1.0, 0.0)
    live_col = jnp.where(iota((EDGES, ROWS), 0) < live, 1.0 / NEG, 0.0)
    which = lax.shift_right_logical(dst_rows[...], 7) & (HALVES - 1)
    which_col = column(which)
    which_col = jnp.concatenate([which_col, which_col], axis=1)
    for b in range(REP):
        dscale[b] = cnts[b, 0:1, :] * live_col
    for h in range(HALVES):
        sscale[h] = jnp.where(which_col == float(h), cnts[REP, 0:1, :] * live_col, 0.0)

    for k in range(CHUNKS):
        ent_copies[k].start()

    def along_x(n):
        return device(0, n, 0, c)

    def along_y(n):
        return device(0, 0, n, c)

    def same(ref, sends, recvs, n, peer):
        return remote(ref, ref, sends.at[n], recvs.at[n], peer)

    def near_one(n, dx):
        return same(gn.at[c, x_at(dx), y], n1_s, n1_r, n, along_x(n))

    def near_line(n, dy):
        return same(gn.at[c, :, y_at(dy)], n2_s, n2_r, n, along_y(n))

    def far_one(n, dy):
        return same(gf.at[c, x, y_at(dy)], f1_s, f1_r, n, along_y(n))

    def far_line(n, dx):
        return same(gf.at[c, x_at(dx)], f2_s, f2_r, n, along_x(n))

    def near_core(n, core):
        return same(gn.at[core], gn_s, gn_r, n, mate)

    def far_core(n, core):
        return same(gf.at[core, x_at(-n)], gf_s, gf_r, n, mate)

    def parts_of(k):
        at = lax.shift_right_logical(k, 4)
        s = k & 15
        kind = lax.shift_right_logical(s * 13, 6)
        r = at * REL_DEV + s - kind * REL_DEV
        near = jnp.where((kind < 3) & (r < NR), kind * NR + r, -1)
        distant = jnp.where(r < NR, -1, kind * FR + r - NR)
        return near, jnp.where(kind == 3, 3 * FR + at, distant)

    @pl.loop(1, NEAR_Z)
    def _(n):
        tile_arrival(n).wait_recv()

    shape = (NEAR_ROWS, NEAR_Z * TILE)
    pick = one_hot(iota(shape, 0) == parts_of(iota(shape, 1))[0])
    gn[c, x, y] = nn(pick, zt[0 : NEAR_Z * TILE, :]).astype(BF)
    for n in range(1, X):
        near_one(n, 0).start()

    @pl.loop(NEAR_Z, Z)
    def _(n):
        tile_arrival(n).wait_recv()

    shape = (FAR_ROWS, SLOTS)
    pick = one_hot(iota(shape, 0) == parts_of(iota(shape, 1))[1])
    gf[c, x, y] = nn(pick, zt[...]).astype(BF)
    for n in range(1, Y):
        far_one(n, 0).start()
    for n in range(1, X):
        near_one(n, -n).wait_recv()
    for n in range(1, Y):
        near_line(n, 0).start()
    for n in range(1, Y):
        far_one(n, -n).wait_recv()
    for n in range(1, X):
        far_line(n, 0).start()
    far_core(0, c).start()
    for n in range(1, Y):
        near_line(n, -n).wait_recv()
    near_core(0, c).start()

    at_y = (1 - yh) * CORES + c
    at_mate = yh * CORES + cm
    at_both = (1 - yh) * CORES + cm

    def entity_copy(k, at, sends, recvs, peer):
        ref = part.at[(at, *piece(k))]
        return remote(ref, ref, sends.at[k], recvs.at[k], peer)

    def entity_on(k):
        ent_copies[k].wait_recv()
        entity_copy(k, rep, y_s, y_r, across).start()
        entity_copy(k, rep, m_s, m_r, mate).start()

    def entity_over(k):
        entity_copy(k, at_y, y_s, y_r, across).wait_recv()
        entity_copy(k, at_y, d_s, d_r, mate).start()

    entity_on(0)
    entity_on(1)
    entity_over(0)
    for n in range(1, X):
        far_line(n, -n).wait_recv()
        far_core(n, c).start()
    entity_over(1)
    entity_on(2)
    near_core(0, cm).wait_recv()
    for n in range(X):
        far_core(n, cm).wait_recv()

    near_table = gn[...].reshape(blocks, NEAR_ROWS, 128)
    far_table = gf[...].reshape(blocks, FAR_ROWS, 128)
    for k in range(3):
        w = nn(ohnt[...], near_table[:, k * NR : (k + 1) * NR, :].reshape(blocks * NR, 128))
        w += nn(ohft[...], far_table[:, k * FR : (k + 1) * FR, :].reshape(blocks * FR, 128))
        wf[k * 128 : (k + 1) * 128, :] = jnp.transpose(w)
    w = nn(ohzt[...], far_table[:, 3 * FR :, :].reshape(blocks * Z, 128))
    fold = one_hot(
        ((iota((128, 128), 0) & 15) == iota((128, 128), 1)) & (iota((128, 128), 0) < 16 * REL_DEV)
    )
    w = nn(jnp.where(slot_mask, w, 0.0).astype(BF), fold)
    wf[384:512, :] = jnp.transpose(w)

    def parts(ref, k):
        re = pl.ds(pl.multiple_of(k * STEP, 8), STEP)
        im = pl.ds(pl.multiple_of(HALF + k * STEP, 8), STEP)
        return ref[re, :], ref[im, :]

    def put(ref, k, re_value, im_value):
        ref[pl.ds(pl.multiple_of(k * STEP, 8), STEP), :] = re_value
        ref[pl.ds(pl.multiple_of(HALF + k * STEP, 8), STEP), :] = im_value

    @pl.loop(0, STEPS)
    def _(k):
        s_re, s_im = parts(sf, k)
        w_re, w_im = parts(wf, k)
        put(qf, k, s_re * w_re - s_im * w_im, s_re * w_im + s_im * w_re)

    qb[...] = qf[0:D, :].astype(BF)
    for k in range(PAD // 128):
        at = slice(k * 128, (k + 1) * 128)
        qrow[:, at] = jnp.transpose(qf[at, :]).astype(BF)

    def half(h):
        lanes = slice(h * 128, (h + 1) * 128)
        for k in range(h * PER_HALF, (h + 1) * PER_HALF):
            entity_copy(k, at_mate, m_s, m_r, mate).wait_recv()
            entity_copy(k, at_both, d_s, d_r, mate).wait_recv()
        total = nn(part[0, 0:D, lanes], ohd[0, lanes, :])
        for b in range(1, REP):
            total += nn(part[b, 0:D, lanes], ohd[b, lanes, :])
        of[...] = total

        def turn(k, positive):
            w_re, w_im = parts(wf, k)
            o_re, o_im = parts(of, k)
            q_re, q_im = parts(qf, k)
            put(uf, k, w_re * o_re + w_im * o_im, w_re * o_im - w_im * o_re)
            return positive + jnp.sum(q_re * o_re + q_im * o_im, axis=0, keepdims=True)

        positive = lax.fori_loop(0, STEPS, turn, jnp.zeros((1, EDGES), F32))
        grad_pos = jnp.where(which == h, -live_row * jax.nn.sigmoid(-positive), 0.0)
        ub[h] = uf[0:D, :].astype(BF)
        for k in range(PAD // 128):
            at = slice(k * 128, (k + 1) * 128)
            urow[:, at] = jnp.transpose(uf[at, :]).astype(BF)
        gs[h] = (jax.nn.sigmoid(nn(urow[...], eb[...])) * sscale[h]).astype(BF)
        for b in range(REP):
            scores = nn(qrow[...], part[b, :, lanes])
            gmat[b, :, lanes] = (jax.nn.sigmoid(scores) * dscale[b, :, lanes]).astype(BF)
        dpf[...] = nt(eb[0:D, :], gs[h])
        total = nt(part[0, 0:D, lanes], gmat[0, :, lanes])
        for b in range(1, REP):
            total += nt(part[b, 0:D, lanes], gmat[b, :, lanes])
        dqf[...] = total

        @pl.loop(0, STEPS)
        def _(k):
            s_re, s_im = parts(sf, k)
            w_re, w_im = parts(wf, k)
            o_re, o_im = parts(of, k)
            q_re, q_im = parts(qf, k)
            u_re, u_im = parts(uf, k)
            dq_re, dq_im = parts(dqf, k)
            dp_re, dp_im = parts(dpf, k)
            dq_re += grad_pos * o_re
            dq_im += grad_pos * o_im
            dp_re += grad_pos * s_re
            dp_im += grad_pos * s_im
            put(
                dof, k,
                grad_pos * q_re + w_re * dp_re - w_im * dp_im,
                grad_pos * q_im + w_re * dp_im + w_im * dp_re,
            )
            dw_re = s_re * dq_re + s_im * dq_im + o_re * dp_re + o_im * dp_im
            dw_im = s_re * dq_im - s_im * dq_re + o_im * dp_re - o_re * dp_im
            ds_re = w_re * dq_re + w_im * dq_im + grad_pos * u_re
            ds_im = w_re * dq_im - w_im * dq_re + grad_pos * u_im
            if h:
                before_re, before_im = parts(dwf, k)
                dw_re += before_re
                dw_im += before_im
                before_re, before_im = parts(dsf, k)
                ds_re += before_re
                ds_im += before_im
            put(dwf, k, dw_re, dw_im)
            put(dsf, k, ds_re, ds_im)

        dob[h] = dof[...].astype(BF)

    def dc_copy(k):
        f, rows = piece(k)
        return remote(dest.at[cm, :, f, rows], dcr.at[:, f, rows], dc_s.at[k], dc_r.at[k], mate)

    def dy_copy(k):
        return remote(ysend.at[piece(k)], yrecv.at[piece(k)], dy_s.at[k], dy_r.at[k], across)

    def dz_copy(k):
        return remote(ezs.at[piece(k)], ezr.at[piece(k)], dz_s.at[k], dz_r.at[k], far)

    def dest_chunk(k):
        f, rows = slices(k)
        h = PIECES[k][2]
        for b in range(REP):
            dest[b % CORES, b // CORES, f, rows] = (
                nn(qb[f, :], gmat[b, :, rows]) + nt(dob[h, f, :], ohd[b, rows, :])
            ).astype(BF)
        dc_copy(k).start()

    def dest_across(k):
        f, rows = slices(k)
        dc_copy(k).wait_recv()
        mine = dest[c, 1 - yh, f, rows].astype(F32) + dcr[1 - yh, f, rows].astype(F32)
        ysend[f, rows] = mine.astype(BF)
        dy_copy(k).start()

    def dest_home(k):
        f, rows = slices(k)
        mine = dest[c, yh, f, rows].astype(F32) + dcr[yh, f, rows].astype(F32)
        dy_copy(k).wait_recv()
        ezs[f, rows] = (mine + yrecv[f, rows].astype(F32)).astype(BF)
        dz_copy(k).start()

    def rel_far(core, n):
        rows = nn(ohf[core, n * Y * FR : (n + 1) * Y * FR, :], dwb[...]).astype(BF)
        ends = nn(ohz[core, n * Y * Z : (n + 1) * Y * Z, :], dwz[...]).astype(BF)
        for m in range(Y):
            for k in range(3):
                rf[core, n, m, k * FR : (k + 1) * FR, :] = rows[
                    m * FR : (m + 1) * FR, k * 128 : (k + 1) * 128
                ]
            rf[core, n, m, 3 * FR :, :] = ends[m * Z : (m + 1) * Z, :]

    def rel_near(core, n):
        rows = nn(ohn[core, n * Y * NR : (n + 1) * Y * NR, :], dwb[...]).astype(BF)
        for m in range(Y):
            for k in range(3):
                rn[core, n, m, k * NR : (k + 1) * NR, :] = rows[
                    m * NR : (m + 1) * NR, k * 128 : (k + 1) * 128
                ]

    def rc_near(n):
        return remote(rn.at[cm], rcn, rcn_s.at[n], rcn_r.at[n], mate)

    def rc_far(n):
        return remote(rf.at[cm, n], rcf.at[n], rcf_s.at[n], rcf_r.at[n], mate)

    def x_first(n):
        ref = rf.at[c, x_at(n), :, 0:FH]
        return remote(ref, rx1.at[n], rx1_s.at[n], rx1_r.at[n], along_x(n))

    def x_second(n):
        return remote(sx.at[y_at(n)], rx2.at[n], rx2_s.at[n], rx2_r.at[n], along_y(n))

    def y_first(n):
        ref = rf.at[c, :, y_at(n), FH:FAR_ROWS]
        return remote(ref, ry1.at[n], ry1_s.at[n], ry1_r.at[n], along_y(n))

    def y_second(n):
        return remote(sy.at[x_at(n)], ry2.at[n], ry2_s.at[n], ry2_r.at[n], along_x(n))

    def near_first(n):
        return remote(rn.at[c, :, y_at(n)], rn1.at[n], rn1_s.at[n], rn1_r.at[n], along_y(n))

    def near_second(n):
        return remote(sn.at[x_at(n)], rn2.at[n], rn2_s.at[n], rn2_r.at[n], along_x(n))

    def far_to_plane():
        for n in range(X):
            rc_far(n).wait_recv()
        for n in [*range(1, X), 0]:
            at = x_at(n)
            rf[c, at] = (rf[c, at].astype(F32) + rcf[at].astype(F32)).astype(BF)
            if n:
                x_first(n).start()
        for n in range(1, Y):
            y_first(n).start()

    def near_to_y():
        rc_near(0).wait_recv()
        for n in [*range(1, Y), 0]:
            at = y_at(n)
            rn[c, :, at] = (rn[c, :, at].astype(F32) + rcn[:, at].astype(F32)).astype(BF)
            if n:
                near_first(n).start()

    def far_turn():
        for n in range(1, X):
            x_first(n).wait_recv()
        for n in [*range(1, Y), 0]:
            at = y_at(n)
            total = rf[c, x, at, 0:FH, :].astype(F32)
            for m in range(1, X):
                total += rx1[m, at].astype(F32)
            sx[at] = total.astype(BF)
            if n:
                x_second(n).start()
        for n in range(1, Y):
            y_first(n).wait_recv()
        for n in [*range(1, X), 0]:
            at = x_at(n)
            total = rf[c, at, y, FH:FAR_ROWS, :].astype(F32)
            for m in range(1, Y):
                total += ry1[m, at].astype(F32)
            sy[at] = total.astype(BF)
            if n:
                y_second(n).start()

    def near_to_x():
        for n in range(1, Y):
            near_first(n).wait_recv()
        for n in [*range(1, X), 0]:
            at = x_at(n)
            total = rn[c, at, y].astype(F32)
            for m in range(1, Y):
                total += rn1[m, at].astype(F32)
            sn[at] = total.astype(BF)
            if n:
                near_second(n).start()

    def rz_copy(n):
        at = slot_there(n)
        return remote(zsend.at[tile_of(n)], zrecv.at[at], rz_s.at[n], rz_r.at[at], slot_device(n))

    def rz_arrival(n):
        return remote(zsend.at[tile_of(n)], zrecv.at[n], rz_s.at[n], rz_r.at[n], slot_device(n))

    half(0)
    dest_chunk(0)
    dest_chunk(1)
    entity_over(2)
    dest_across(0)
    dest_across(1)
    entity_on(3)
    dest_home(0)
    dest_home(1)
    entity_over(3)
    half(1)
    dest_chunk(2)
    dest_chunk(3)
    for k in range(3):
        dwb[:, k * 128 : (k + 1) * 128] = jnp.transpose(dwf[k * 128 : (k + 1) * 128, :]).astype(BF)
    spread = one_hot(
        ((iota((128, 128), 1) & 15) == iota((128, 128), 0)) & (iota((128, 128), 1) < 16 * REL_DEV)
    )
    tail = nn(jnp.transpose(dwf[384:512, :]).astype(BF), spread)
    dwz[...] = jnp.where(slot_mask, tail, 0.0).astype(BF)
    for n in range(X):
        rel_far(cm, n)
        rc_far(n).start()
    for n in range(X):
        rel_near(cm, n)
    rc_near(0).start()
    for n in range(X):
        rel_far(c, n)
    far_to_plane()
    dest_across(2)
    dest_across(3)
    for n in range(X):
        rel_near(c, n)
    near_to_y()
    dest_home(2)
    dest_home(3)
    for k in range(CHUNKS):
        ent_copies[k].wait_send()
        entity_copy(k, rep, y_s, y_r, across).wait_send()
        entity_copy(k, rep, m_s, m_r, mate).wait_send()
        entity_copy(k, at_y, d_s, d_r, mate).wait_send()
    for n in range(X):
        far_core(n, c).wait_send()
    near_core(0, c).wait_send()
    for n in range(1, X):
        near_one(n, 0).wait_send()
        far_line(n, 0).wait_send()
    for n in range(1, Y):
        near_line(n, 0).wait_send()
        far_one(n, 0).wait_send()

    @pl.loop(1, Z)
    def _(n):
        tile_copy(n).wait_send()

    far_turn()
    near_to_x()

    ds_hi = dsf[...].astype(BF)
    ds_lo = (dsf[...] - ds_hi.astype(F32)).astype(BF)
    total = nt(ds_hi, ohs[...]) + nt(ds_lo, ohs[...])
    for h in range(HALVES):
        total += nn(ub[h], gs[h])
    sf[...] = total
    for k in range(CHUNKS):
        dc_copy(k).wait_send()
        dy_copy(k).wait_send()
    for n in range(X):
        rc_far(n).wait_send()
    rc_near(0).wait_send()
    for n in range(1, X):
        x_first(n).wait_send()
    for n in range(1, Y):
        y_first(n).wait_send()
        near_first(n).wait_send()

    total = sx[y].astype(F32)
    for n in range(1, Y):
        x_second(n).wait_recv()
        total += rx2[n].astype(F32)
    other = sy[x].astype(F32)
    for n in range(1, X):
        y_second(n).wait_recv()
        other += ry2[n].astype(F32)
    far_sum = jnp.concatenate([total, other], axis=0).astype(BF)
    shape = (SLOTS, FAR_ROWS)
    pick = one_hot(iota(shape, 1) == parts_of(iota(shape, 0))[1])
    tiles = nn(pick, far_sum)
    zsend[NEAR_Z * TILE :, :] = tiles[NEAR_Z * TILE :, :].astype(BF)

    @pl.loop(NEAR_Z, Z)
    def _(n):
        rz_copy(n).start()

    total = sn[x].astype(F32)
    for n in range(1, X):
        near_second(n).wait_recv()
        total += rn2[n].astype(F32)
    near_sum = total.astype(BF)
    shape = (NEAR_Z * TILE, NEAR_ROWS)
    pick = one_hot(iota(shape, 1) == parts_of(iota(shape, 0))[0])
    zsend[0 : NEAR_Z * TILE, :] = (nn(pick, near_sum) + tiles[0 : NEAR_Z * TILE, :]).astype(BF)

    @pl.loop(1, NEAR_Z)
    def _(n):
        rz_copy(n).start()

    for n in range(1, X):
        y_second(n).wait_send()
        near_second(n).wait_send()
    for n in range(1, Y):
        x_second(n).wait_send()
    for k in range(CHUNKS):
        dz_copy(k).wait_send()

    @pl.loop(1, Z)
    def _(n):
        rz_copy(n).wait_send()

    for k in range(CHUNKS):
        dz_copy(k).wait_recv()
    ent_grad[...] = sf[...] + ezr[...].astype(F32)

    def add_tile(n, acc):
        rz_arrival(n).wait_recv()
        return acc + zrecv[n].astype(F32)

    rel_grad[...] = lax.fori_loop(1, Z, add_tile, zsend[0:TILE, :].astype(F32))


def update(
    ent, state, rel, rel_state, ent_grad, rel_grad, new_ent, new_state, new_rel, new_rel_state
):
    grad = ent_grad[...]
    fresh = state[...] + jnp.sum(grad * grad, axis=0, keepdims=True) * (1.0 / D)
    new_state[...] = fresh
    new_ent[...] = ent[...] - grad * (0.5 / jnp.sqrt(fresh))

    lane = iota((REL_DEV, 128), 1)
    row5 = iota((REL_DEV, 128), 0)
    own_slot = lax.shift_right_logical(lane, 4) == row5
    ends = jnp.where(own_slot, jnp.broadcast_to(rel_grad[15:16, :], (REL_DEV, 128)), 0.0)
    fold_f = jnp.where(
        ((iota((128, 128), 0) & 15) == iota((128, 128), 1)) & (iota((128, 128), 0) < 16 * REL_DEV),
        1.0,
        0.0,
    )
    ends = jnp.dot(ends, fold_f, precision=lax.Precision.HIGHEST, preferred_element_type=F32)
    pieces = [rel_grad[k * REL_DEV : (k + 1) * REL_DEV, :] for k in range(3)] + [ends]
    squares = jnp.sum(sum(piece * piece for piece in pieces), axis=1, keepdims=True)
    eye = iota((REL_DEV, REL_DEV), 0) == iota((REL_DEV, REL_DEV), 1)
    old = jnp.broadcast_to(rel_state[...], (REL_DEV, REL_DEV))
    old = jnp.sum(jnp.where(eye, old, 0.0), axis=1, keepdims=True)
    fresh = old + squares * (1.0 / D)
    new_rel_state[...] = jnp.sum(
        jnp.where(eye, jnp.broadcast_to(fresh, (REL_DEV, REL_DEV)), 0.0), axis=0, keepdims=True
    )
    scale = 0.5 / jnp.sqrt(fresh)
    for k in range(3):
        at = slice(k * 128, (k + 1) * 128)
        new_rel[:, at] = rel[:, at] - pieces[k] * scale
    new_rel[:, 384:400] = rel[:, 384:400] - ends[:, 0:16] * scale


def scratch():
    vm = pltpu.VMEM
    dma = pltpu.SemaphoreType.DMA
    blocks = PI * CORES
    return [
        vm((D, ROWS), F32),
        vm((REL_DEV, D), F32),
        vm((1, EDGES), jnp.int32),
        vm((1, EDGES), jnp.int32),
        vm((1, EDGES), jnp.int32),
        vm((1, NEG), jnp.int32),
        vm((1, NEG), jnp.int32),
        vm((PAD, ROWS), BF),
        vm((REP, PAD, ROWS), BF),
        vm((SLOTS, 128), BF),
        vm((CORES, X, Y, NEAR_ROWS, 128), BF),
        vm((CORES, X, Y, FAR_ROWS, 128), BF),
        vm((TILE, 128), F32),
        vm((ROWS, EDGES), BF),
        vm((REP, ROWS, EDGES), BF),
        vm((CORES, PI * NR, EDGES), BF),
        vm((CORES, PI * FR, EDGES), BF),
        vm((CORES, PI * Z, EDGES), BF),
        vm((EDGES, blocks * NR), BF),
        vm((EDGES, blocks * FR), BF),
        vm((EDGES, blocks * Z), BF),
        vm((2, NEG_PAD), jnp.int32),
        vm((REP + 1, 16, ROWS), F32),
        vm((D, EDGES), F32),
        vm((PAD, EDGES), F32),
        vm((D, EDGES), F32),
        vm((PAD, EDGES), F32),
        vm((PAD, EDGES), F32),
        vm((D, EDGES), F32),
        vm((D, EDGES), F32),
        vm((D, EDGES), F32),
        vm((D, EDGES), F32),
        vm((PAD, EDGES), F32),
        vm((D, EDGES), BF),
        vm((EDGES, PAD), BF),
        vm((EDGES, PAD), BF),
        vm((REP, EDGES, ROWS), BF),
        vm((HALVES, EDGES, ROWS), BF),
        vm((HALVES, D, EDGES), BF),
        vm((HALVES, D, EDGES), BF),
        vm((HALVES, EDGES, ROWS), F32),
        vm((REP, EDGES, ROWS), F32),
        vm((EDGES, 384), BF),
        vm((EDGES, 128), BF),
        vm((CORES, YH, D, ROWS), BF),
        vm((YH, D, ROWS), BF),
        vm((D, ROWS), BF),
        vm((D, ROWS), BF),
        vm((D, ROWS), BF),
        vm((D, ROWS), BF),
        vm((CORES, X, Y, NEAR_ROWS, 128), BF),
        vm((CORES, X, Y, FAR_ROWS, 128), BF),
        vm((X, Y, NEAR_ROWS, 128), BF),
        vm((X, Y, FAR_ROWS, 128), BF),
        vm((Y, X, NEAR_ROWS, 128), BF),
        vm((X, NEAR_ROWS, 128), BF),
        vm((X, Y, FH, 128), BF),
        vm((Y, FH, 128), BF),
        vm((Y, X, FH, 128), BF),
        vm((X, FH, 128), BF),
        vm((X, NEAR_ROWS, 128), BF),
        vm((Y, FH, 128), BF),
        vm((X, FH, 128), BF),
        vm((SLOTS, 128), BF),
        vm((Z, TILE, 128), BF),
    ] + [
        dma((n,))
        for n in [Z] * 2 + [CHUNKS] * 8 + [max(X, Y)] * 12 + [CHUNKS] * 6 + [max(X, Y)] * 16 + [Z] * 2
    ] + [dma((7,))]


def local(
    entities, ent_state, relations, rel_state, src_rows, dst_rows, rel_ids, neg_src, neg_dst, edge_count
):
    vmem = pl.BlockSpec(memory_space=pltpu.VMEM)
    ent = entities.T
    ent_grad, rel_grad = pl.pallas_call(
        kernel,
        out_shape=(
            jax.ShapeDtypeStruct((D, ROWS), F32),
            jax.ShapeDtypeStruct((TILE, 128), F32),
        ),
        in_specs=[pl.BlockSpec(memory_space=pl.ANY)] * 7 + [vmem],
        out_specs=(vmem,) * 2,
        scratch_shapes=scratch(),
        compiler_params=pltpu.CompilerParams(
            collective_id=0, has_side_effects=True, vmem_limit_bytes=56 * 1024 * 1024
        ),
        name="bucket_round",
    )(
        ent, relations, src_rows, dst_rows, rel_ids, neg_src, neg_dst, edge_count.reshape(1, 1)
    )
    new_ent, new_state, new_rel, new_rel_state = pl.pallas_call(
        update,
        out_shape=(
            jax.ShapeDtypeStruct((D, ROWS), F32),
            jax.ShapeDtypeStruct((1, ROWS), F32),
            jax.ShapeDtypeStruct((REL_DEV, D), F32),
            jax.ShapeDtypeStruct((1, REL_DEV), F32),
        ),
        in_specs=[vmem] * 6,
        out_specs=(vmem,) * 4,
        name="row_update",
    )(
        ent,
        ent_state.reshape(1, ROWS),
        relations,
        rel_state.reshape(1, REL_DEV),
        ent_grad,
        rel_grad,
    )
    return (new_ent.T, new_state.reshape(ROWS), new_rel, new_rel_state.reshape(REL_DEV))


def solution(mesh):
    rows = P(("dom", "rep"), None)
    flat = P(("dom", "rep"))
    return jax.shard_map(
        local,
        mesh=mesh,
        in_specs=(rows, flat, rows, flat, rows, rows, rows, rows, rows, flat),
        out_specs=(rows, flat, rows, flat),
        check_vma=False,
    )
```

```python
import jax
import jax.numpy as jnp
from jax import lax
from jax.experimental import pallas as pl
from jax.experimental.pallas import tpu as pltpu
from jax.sharding import PartitionSpec as P

Z, X, YL, YH, CORES = 16, 4, 2, 2, 2
Y = YL * YH
PI = X * Y
D = 400
HALF = D // 2
PAD = 512
ROWS = 256
EDGES = 256
NEG = 1000
NEG_PAD = 1024
REP = YH * CORES
REL_DEV = 5
TILE = 16
SLOTS = Z * TILE
CB = Z * REL_DEV
NR = 2 * Z
FR = CB - NR
NEAR_Z = -(-NR // REL_DEV)
NEAR_ROWS = 3 * NR
FAR_ROWS = 3 * FR + Z
FH = FAR_ROWS // 2
HALVES = ROWS // 128
SPLIT = 208
PIECES = [(0, D, 0), (0, SPLIT, 1), (SPLIT, D - SPLIT, 1)]
CHUNKS = len(PIECES)
STEP = 40
STEPS = HALF // STEP
SHIFT_PLANE = (PI * CORES).bit_length() - 1
SHIFT_CORE = CORES.bit_length() - 1
SHIFT_YH = SHIFT_CORE + YH.bit_length() - 1
SHIFT_YL = SHIFT_YH + YL.bit_length() - 1
BF = jnp.bfloat16
F32 = jnp.float32
MESH = pl.DeviceIdType.MESH


def nn(a, b):
    return jnp.dot(a, b, preferred_element_type=F32)


def nt(a, b):
    return lax.dot_general(a, b, (((1,), (1,)), ((), ())), preferred_element_type=F32)


def iota(shape, dim):
    return lax.broadcasted_iota(jnp.int32, shape, dim)


def one_hot(cond):
    return jnp.where(cond, 1.0, 0.0).astype(BF)


def div5(v):
    return lax.shift_right_logical(v * 52429, 18)


def remote(src, dst, send, recv, peer):
    return pltpu.make_async_remote_copy(
        src_ref=src, dst_ref=dst, send_sem=send, recv_sem=recv, device_id=peer, device_id_type=MESH
    )


def kernel(
    ent, rel_in, src_in, dst_in, ids_in, neg_src_in, neg_dst_in, count,
    ent_grad, rel_grad,
    ent_here, rel, src_rows, dst_rows, rel_ids, neg_src, neg_dst, eb, part, zt, gn, gf, tf, ohs, ohd, ohn, ohf, ohz, ohnt, ohft, ohzt, negs, cnts,
    sf, wf, of, qf, uf, dqf, dpf, dof, dsf, dwf,
    qb, qrow, urow, gmat, gs, dob, ub, sscale, dscale, dwb, dwz,
    dest, dcr, ysend, yrecv, ezs, ezr, rn, rf, rcn, rcf, rn1, rn2, rx1, rx2, ry1, ry2, sn, sx, sy, zsend, zrecv,
    zt_s, zt_r, e_s, e_r, y_s, y_r, m_s, m_r, d_s, d_r, n1_s, n1_r, n2_s, n2_r, f1_s, f1_r, f2_s, f2_r, gn_s, gn_r, gf_s, gf_r,
    dc_s, dc_r, dy_s, dy_r, dz_s, dz_r, rcn_s, rcn_r, rcf_s, rcf_r, rn1_s, rn1_r, rn2_s, rn2_r, rx1_s, rx1_r, rx2_s, rx2_r, ry1_s, ry1_r, ry2_s, ry2_r,
    rz_s, rz_r, in_sem,
):
    dom = lax.axis_index("dom")
    rep = lax.axis_index("rep")
    z = dom // (X * YL)
    x = (dom // YL) % X
    yl = dom % YL
    yh = rep // CORES
    c = rep % CORES
    y = yh * YL + yl
    cm = 1 - c

    def device(dz, dx, dy, core):
        yy = (y + dy) % Y
        return {
            "dom": (((z + dz) % Z) * X + (x + dx) % X) * YL + yy % YL,
            "rep": (yy // YL) * CORES + core,
        }

    def x_at(n):
        return (x + X + n) % X

    def y_at(n):
        return (y + Y + n) % Y

    mate = device(0, 0, 0, cm)
    across = device(0, 0, YL, c)
    far = device(Z // 2, 0, 0, c)

    reads = [
        pltpu.make_async_copy(source, here, in_sem.at[n])
        for n, (source, here) in enumerate(
            (
                (rel_in, rel),
                (ent, ent_here),
                (src_in, src_rows),
                (dst_in, dst_rows),
                (ids_in, rel_ids),
                (neg_src_in, neg_src),
                (neg_dst_in, neg_dst),
            )
        )
    ]

    barrier = pltpu.get_barrier_semaphore()

    @pl.loop(1, Z)
    def _(n):
        pl.semaphore_signal(barrier, inc=1, device_id=device(n, 0, 0, c), device_id_type=MESH)

    for n in range(1, X):
        pl.semaphore_signal(barrier, inc=1, device_id=device(0, n, 0, c), device_id_type=MESH)
    for n in range(1, Y):
        pl.semaphore_signal(barrier, inc=1, device_id=device(0, 0, n, c), device_id_type=MESH)
    pl.semaphore_signal(barrier, inc=1, device_id=mate, device_id_type=MESH)

    for read in reads:
        read.start()

    reads[0].wait()
    lane = iota((REL_DEV, 128), 1)
    row5 = iota((REL_DEV, 128), 0)
    for k in range(3):
        tf[k * REL_DEV : (k + 1) * REL_DEV, :] = rel[:, k * 128 : (k + 1) * 128]
    spread16 = one_hot((iota((16, 128), 1) & 15) == iota((16, 128), 0))
    last = nn(rel[:, 384:400].astype(BF), spread16)
    last = jnp.where(lax.shift_right_logical(lane, 4) == row5, last, 0.0)
    tf[15:16, :] = jnp.sum(last, axis=0, keepdims=True)
    zt[0:TILE, :] = tf[...].astype(BF)

    pl.semaphore_wait(barrier, (Z - 1) + (X - 1) + (Y - 1) + 1)

    def slot_device(n):
        return device(jnp.where(n % 2 == 1, (n + 1) // 2, Z - n // 2), 0, 0, c)

    def slot_there(n):
        return jnp.where(n % 2 == 1, jnp.minimum(n + 1, Z - 1), n - 1) if Z > 2 else n

    def tile_of(n):
        return pl.ds(pl.multiple_of(n * TILE, TILE), TILE)

    def tile_copy(n):
        at = slot_there(n)
        return remote(
            zt.at[tile_of(0)], zt.at[tile_of(at)], zt_s.at[n], zt_r.at[at], slot_device(n)
        )

    def tile_arrival(n):
        return remote(zt.at[tile_of(n)], zt.at[tile_of(n)], zt_s.at[n], zt_r.at[n], slot_device(n))

    @pl.loop(NEAR_Z, Z)
    def _(n):
        tile_copy(n).start()

    @pl.loop(1, NEAR_Z)
    def _(n):
        tile_copy(n).start()

    def piece(k):
        at, size, h = PIECES[k]
        return pl.ds(at, size), pl.ds(h * 128, 128)

    def slices(k):
        at, size, h = PIECES[k]
        return slice(at, at + size), slice(h * 128, (h + 1) * 128)

    ent_copies = [
        remote(eb.at[piece(k)], part.at[(rep, *piece(k))], e_s.at[k], e_r.at[k], far)
        for k in range(CHUNKS)
    ]

    for read in reads[1:]:
        read.wait()
    eb[0:D, :] = ent_here[...].astype(BF)
    part[:, D:PAD, :] = jnp.zeros((REP, PAD - D, ROWS), BF)
    eb[D:PAD, :] = jnp.zeros((PAD - D, ROWS), BF)
    qf[D:PAD, :] = jnp.zeros((PAD - D, EDGES), F32)
    uf[D:PAD, :] = jnp.zeros((PAD - D, EDGES), F32)
    dwf[D:PAD, :] = jnp.zeros((PAD - D, EDGES), F32)
    ids = rel_ids[...]
    owner = div5(ids)
    slot = ids - owner * REL_DEV
    owner_z = lax.shift_right_logical(owner, SHIFT_PLANE)
    owner_p = owner & (PI * CORES - 1)
    owner_yh = lax.shift_right_logical(owner_p, SHIFT_CORE) & (YH - 1)
    owner_yl = lax.shift_right_logical(owner_p, SHIFT_YH) & (YL - 1)
    owner_x = lax.shift_right_logical(owner_p, SHIFT_YL)
    block = (((owner_p & (CORES - 1)) * X + owner_x) * YH + owner_yh) * YL + owner_yl
    ring = (owner_z + Z - z) & (Z - 1)
    order = jnp.where(ring * 2 <= Z, jnp.maximum(2 * ring - 1, 0), 2 * (Z - ring))
    row = order * REL_DEV + slot
    pos_n = jnp.where(row < NR, block * NR + row, -1)
    pos_f = jnp.where(row < NR, -1, block * FR + row - NR)
    pos_z = block * Z + order

    ohs[...] = one_hot(iota((ROWS, EDGES), 0) == src_rows[...])
    for b in range(REP):
        ohd[b] = one_hot(iota((ROWS, EDGES), 0) + b * ROWS == dst_rows[...])

    def column(row):
        return jnp.transpose(jnp.broadcast_to(row.astype(F32), (EDGES, EDGES)))[:, :128]

    slot_col = column(slot)
    blocks = PI * CORES
    lanes = iota((EDGES, 128), 1).astype(F32)
    for count_at, at, hot, hot_t in (
        (NR, pos_n, ohn, ohnt),
        (FR, pos_f, ohf, ohft),
        (Z, pos_z, ohz, ohzt),
    ):

        @pl.loop(0, PI)
        def _(n):
            for k in range(CORES):
                hot[k, pl.ds(pl.multiple_of(n * count_at, 16), count_at), :] = one_hot(
                    iota((count_at, EDGES), 0) + (k * PI + n) * count_at == at
                )

        at_col = column(at)
        for t in range(0, blocks * count_at, 128):
            value = one_hot(lanes + float(t) == at_col)
            hot_t[:, t : t + 128] = value[:, : min(128, blocks * count_at - t)]
    slot_mask = lax.shift_right_logical(iota((EDGES, 128), 1), 4).astype(F32) == slot_col

    ones = jnp.ones((16, NEG_PAD), BF)
    negs[...] = jnp.full((2, NEG_PAD), -1, jnp.int32)
    negs[0:1, 0:NEG] = neg_dst[...]
    negs[1:2, 0:NEG] = neg_src[...]
    for b in range(REP):
        cnts[b] = nt(ones, one_hot(iota((ROWS, NEG_PAD), 0) + b * ROWS == negs[0:1, :]))
    cnts[REP] = nt(ones, one_hot(iota((ROWS, NEG_PAD), 0) == negs[1:2, :]))
    sf[...] = nn(eb[0:D, :], ohs[...])

    live = count[...]
    live_row = jnp.where(iota((1, EDGES), 1) < live, 1.0, 0.0)
    live_col = jnp.where(iota((EDGES, ROWS), 0) < live, 1.0 / NEG, 0.0)
    which = lax.shift_right_logical(dst_rows[...], 7) & (HALVES - 1)
    which_col = column(which)
    which_col = jnp.concatenate([which_col, which_col], axis=1)
    for b in range(REP):
        dscale[b] = cnts[b, 0:1, :] * live_col
    for h in range(HALVES):
        sscale[h] = jnp.where(which_col == float(h), cnts[REP, 0:1, :] * live_col, 0.0)

    for k in range(CHUNKS):
        ent_copies[k].start()

    def along_x(n):
        return device(0, n, 0, c)

    def along_y(n):
        return device(0, 0, n, c)

    def same(ref, sends, recvs, n, peer):
        return remote(ref, ref, sends.at[n], recvs.at[n], peer)

    def near_one(n, dx):
        return same(gn.at[c, x_at(dx), y], n1_s, n1_r, n, along_x(n))

    def near_line(n, dy):
        return same(gn.at[c, :, y_at(dy)], n2_s, n2_r, n, along_y(n))

    def far_one(n, dy):
        return same(gf.at[c, x, y_at(dy)], f1_s, f1_r, n, along_y(n))

    def far_line(n, dx):
        return same(gf.at[c, x_at(dx)], f2_s, f2_r, n, along_x(n))

    def near_core(n, core):
        return same(gn.at[core], gn_s, gn_r, n, mate)

    def far_core(n, core):
        return same(gf.at[core, x_at(-n)], gf_s, gf_r, n, mate)

    def parts_of(k):
        at = lax.shift_right_logical(k, 4)
        s = k & 15
        kind = lax.shift_right_logical(s * 13, 6)
        r = at * REL_DEV + s - kind * REL_DEV
        near = jnp.where((kind < 3) & (r < NR), kind * NR + r, -1)
        distant = jnp.where(r < NR, -1, kind * FR + r - NR)
        return near, jnp.where(kind == 3, 3 * FR + at, distant)

    @pl.loop(1, NEAR_Z)
    def _(n):
        tile_arrival(n).wait_recv()

    shape = (NEAR_ROWS, NEAR_Z * TILE)
    pick = one_hot(iota(shape, 0) == parts_of(iota(shape, 1))[0])
    gn[c, x, y] = nn(pick, zt[0 : NEAR_Z * TILE, :]).astype(BF)
    for n in range(1, X):
        near_one(n, 0).start()

    @pl.loop(NEAR_Z, Z)
    def _(n):
        tile_arrival(n).wait_recv()

    shape = (FAR_ROWS, SLOTS)
    pick = one_hot(iota(shape, 0) == parts_of(iota(shape, 1))[1])
    gf[c, x, y] = nn(pick, zt[...]).astype(BF)
    for n in range(1, Y):
        far_one(n, 0).start()
    for n in range(1, X):
        near_one(n, -n).wait_recv()
    for n in range(1, Y):
        near_line(n, 0).start()
    for n in range(1, Y):
        far_one(n, -n).wait_recv()
    for n in range(1, X):
        far_line(n, 0).start()
    far_core(0, c).start()
    for n in range(1, Y):
        near_line(n, -n).wait_recv()
    near_core(0, c).start()

    at_y = (1 - yh) * CORES + c
    at_mate = yh * CORES + cm
    at_both = (1 - yh) * CORES + cm

    def entity_copy(k, at, sends, recvs, peer):
        ref = part.at[(at, *piece(k))]
        return remote(ref, ref, sends.at[k], recvs.at[k], peer)

    def entity_on(k):
        ent_copies[k].wait_recv()
        entity_copy(k, rep, y_s, y_r, across).start()
        entity_copy(k, rep, m_s, m_r, mate).start()

    def entity_over(k):
        entity_copy(k, at_y, y_s, y_r, across).wait_recv()
        entity_copy(k, at_y, d_s, d_r, mate).start()

    entity_on(0)
    entity_over(0)
    for n in range(1, X):
        far_line(n, -n).wait_recv()
        far_core(n, c).start()
    entity_on(1)
    near_core(0, cm).wait_recv()
    for n in range(X):
        far_core(n, cm).wait_recv()

    near_table = gn[...].reshape(blocks, NEAR_ROWS, 128)
    far_table = gf[...].reshape(blocks, FAR_ROWS, 128)
    for k in range(3):
        w = nn(ohnt[...], near_table[:, k * NR : (k + 1) * NR, :].reshape(blocks * NR, 128))
        w += nn(ohft[...], far_table[:, k * FR : (k + 1) * FR, :].reshape(blocks * FR, 128))
        wf[k * 128 : (k + 1) * 128, :] = jnp.transpose(w)
    w = nn(ohzt[...], far_table[:, 3 * FR :, :].reshape(blocks * Z, 128))
    fold = one_hot(
        ((iota((128, 128), 0) & 15) == iota((128, 128), 1)) & (iota((128, 128), 0) < 16 * REL_DEV)
    )
    w = nn(jnp.where(slot_mask, w, 0.0).astype(BF), fold)
    wf[384:512, :] = jnp.transpose(w)

    def parts(ref, k):
        re = pl.ds(pl.multiple_of(k * STEP, 8), STEP)
        im = pl.ds(pl.multiple_of(HALF + k * STEP, 8), STEP)
        return ref[re, :], ref[im, :]

    def put(ref, k, re_value, im_value):
        ref[pl.ds(pl.multiple_of(k * STEP, 8), STEP), :] = re_value
        ref[pl.ds(pl.multiple_of(HALF + k * STEP, 8), STEP), :] = im_value

    @pl.loop(0, STEPS)
    def _(k):
        s_re, s_im = parts(sf, k)
        w_re, w_im = parts(wf, k)
        put(qf, k, s_re * w_re - s_im * w_im, s_re * w_im + s_im * w_re)

    qb[...] = qf[0:D, :].astype(BF)
    for k in range(PAD // 128):
        at = slice(k * 128, (k + 1) * 128)
        qrow[:, at] = jnp.transpose(qf[at, :]).astype(BF)

    def half(h):
        lanes = slice(h * 128, (h + 1) * 128)
        for k in (k for k in range(CHUNKS) if PIECES[k][2] == h):
            entity_copy(k, at_mate, m_s, m_r, mate).wait_recv()
            entity_copy(k, at_both, d_s, d_r, mate).wait_recv()
        total = nn(part[0, 0:D, lanes], ohd[0, lanes, :])
        for b in range(1, REP):
            total += nn(part[b, 0:D, lanes], ohd[b, lanes, :])
        of[...] = total

        def turn(k, positive):
            w_re, w_im = parts(wf, k)
            o_re, o_im = parts(of, k)
            q_re, q_im = parts(qf, k)
            put(uf, k, w_re * o_re + w_im * o_im, w_re * o_im - w_im * o_re)
            return positive + jnp.sum(q_re * o_re + q_im * o_im, axis=0, keepdims=True)

        positive = lax.fori_loop(0, STEPS, turn, jnp.zeros((1, EDGES), F32))
        grad_pos = jnp.where(which == h, -live_row * jax.nn.sigmoid(-positive), 0.0)
        ub[h] = uf[0:D, :].astype(BF)
        for k in range(PAD // 128):
            at = slice(k * 128, (k + 1) * 128)
            urow[:, at] = jnp.transpose(uf[at, :]).astype(BF)
        gs[h] = (jax.nn.sigmoid(nn(urow[...], eb[...])) * sscale[h]).astype(BF)
        for b in range(REP):
            scores = nn(qrow[...], part[b, :, lanes])
            gmat[b, :, lanes] = (jax.nn.sigmoid(scores) * dscale[b, :, lanes]).astype(BF)
        dpf[...] = nt(eb[0:D, :], gs[h])
        total = nt(part[0, 0:D, lanes], gmat[0, :, lanes])
        for b in range(1, REP):
            total += nt(part[b, 0:D, lanes], gmat[b, :, lanes])
        dqf[...] = total

        @pl.loop(0, STEPS)
        def _(k):
            s_re, s_im = parts(sf, k)
            w_re, w_im = parts(wf, k)
            o_re, o_im = parts(of, k)
            q_re, q_im = parts(qf, k)
            u_re, u_im = parts(uf, k)
            dq_re, dq_im = parts(dqf, k)
            dp_re, dp_im = parts(dpf, k)
            dq_re += grad_pos * o_re
            dq_im += grad_pos * o_im
            dp_re += grad_pos * s_re
            dp_im += grad_pos * s_im
            put(
                dof, k,
                grad_pos * q_re + w_re * dp_re - w_im * dp_im,
                grad_pos * q_im + w_re * dp_im + w_im * dp_re,
            )
            dw_re = s_re * dq_re + s_im * dq_im + o_re * dp_re + o_im * dp_im
            dw_im = s_re * dq_im - s_im * dq_re + o_im * dp_re - o_re * dp_im
            ds_re = w_re * dq_re + w_im * dq_im + grad_pos * u_re
            ds_im = w_re * dq_im - w_im * dq_re + grad_pos * u_im
            if h:
                before_re, before_im = parts(dwf, k)
                dw_re += before_re
                dw_im += before_im
                before_re, before_im = parts(dsf, k)
                ds_re += before_re
                ds_im += before_im
            put(dwf, k, dw_re, dw_im)
            put(dsf, k, ds_re, ds_im)

        dob[h] = dof[...].astype(BF)

    def dc_copy(k):
        f, rows = piece(k)
        return remote(dest.at[cm, :, f, rows], dcr.at[:, f, rows], dc_s.at[k], dc_r.at[k], mate)

    def dy_copy(k):
        return remote(ysend.at[piece(k)], yrecv.at[piece(k)], dy_s.at[k], dy_r.at[k], across)

    def dz_copy(k):
        return remote(ezs.at[piece(k)], ezr.at[piece(k)], dz_s.at[k], dz_r.at[k], far)

    def dest_chunk(k):
        f, rows = slices(k)
        h = PIECES[k][2]
        for b in range(REP):
            dest[b % CORES, b // CORES, f, rows] = (
                nn(qb[f, :], gmat[b, :, rows]) + nt(dob[h, f, :], ohd[b, rows, :])
            ).astype(BF)
        dc_copy(k).start()

    def dest_across(k):
        f, rows = slices(k)
        dc_copy(k).wait_recv()
        mine = dest[c, 1 - yh, f, rows].astype(F32) + dcr[1 - yh, f, rows].astype(F32)
        ysend[f, rows] = mine.astype(BF)
        dy_copy(k).start()

    def dest_home(k):
        f, rows = slices(k)
        mine = dest[c, yh, f, rows].astype(F32) + dcr[yh, f, rows].astype(F32)
        dy_copy(k).wait_recv()
        ezs[f, rows] = (mine + yrecv[f, rows].astype(F32)).astype(BF)
        dz_copy(k).start()

    def rel_far(core, n):
        rows = nn(ohf[core, n * Y * FR : (n + 1) * Y * FR, :], dwb[...]).astype(BF)
        ends = nn(ohz[core, n * Y * Z : (n + 1) * Y * Z, :], dwz[...]).astype(BF)
        for m in range(Y):
            for k in range(3):
                rf[core, n, m, k * FR : (k + 1) * FR, :] = rows[
                    m * FR : (m + 1) * FR, k * 128 : (k + 1) * 128
                ]
            rf[core, n, m, 3 * FR :, :] = ends[m * Z : (m + 1) * Z, :]

    def rel_near(core, n):
        rows = nn(ohn[core, n * Y * NR : (n + 1) * Y * NR, :], dwb[...]).astype(BF)
        for m in range(Y):
            for k in range(3):
                rn[core, n, m, k * NR : (k + 1) * NR, :] = rows[
                    m * NR : (m + 1) * NR, k * 128 : (k + 1) * 128
                ]

    def rc_near(n):
        return remote(rn.at[cm], rcn, rcn_s.at[n], rcn_r.at[n], mate)

    def rc_far(n):
        return remote(rf.at[cm, n], rcf.at[n], rcf_s.at[n], rcf_r.at[n], mate)

    def x_first(n):
        ref = rf.at[c, x_at(n), :, 0:FH]
        return remote(ref, rx1.at[n], rx1_s.at[n], rx1_r.at[n], along_x(n))

    def x_second(n):
        return remote(sx.at[y_at(n)], rx2.at[n], rx2_s.at[n], rx2_r.at[n], along_y(n))

    def y_first(n):
        ref = rf.at[c, :, y_at(n), FH:FAR_ROWS]
        return remote(ref, ry1.at[n], ry1_s.at[n], ry1_r.at[n], along_y(n))

    def y_second(n):
        return remote(sy.at[x_at(n)], ry2.at[n], ry2_s.at[n], ry2_r.at[n], along_x(n))

    def near_first(n):
        return remote(rn.at[c, :, y_at(n)], rn1.at[n], rn1_s.at[n], rn1_r.at[n], along_y(n))

    def near_second(n):
        return remote(sn.at[x_at(n)], rn2.at[n], rn2_s.at[n], rn2_r.at[n], along_x(n))

    def far_to_plane():
        for n in range(X):
            rc_far(n).wait_recv()
        for n in [*range(1, X), 0]:
            at = x_at(n)
            rf[c, at] = (rf[c, at].astype(F32) + rcf[at].astype(F32)).astype(BF)
            if n:
                x_first(n).start()
        for n in range(1, Y):
            y_first(n).start()

    def near_to_y():
        rc_near(0).wait_recv()
        for n in [*range(1, Y), 0]:
            at = y_at(n)
            rn[c, :, at] = (rn[c, :, at].astype(F32) + rcn[:, at].astype(F32)).astype(BF)
            if n:
                near_first(n).start()

    def far_turn():
        for n in range(1, X):
            x_first(n).wait_recv()
        for n in [*range(1, Y), 0]:
            at = y_at(n)
            total = rf[c, x, at, 0:FH, :].astype(F32)
            for m in range(1, X):
                total += rx1[m, at].astype(F32)
            sx[at] = total.astype(BF)
            if n:
                x_second(n).start()
        for n in range(1, Y):
            y_first(n).wait_recv()
        for n in [*range(1, X), 0]:
            at = x_at(n)
            total = rf[c, at, y, FH:FAR_ROWS, :].astype(F32)
            for m in range(1, Y):
                total += ry1[m, at].astype(F32)
            sy[at] = total.astype(BF)
            if n:
                y_second(n).start()

    def near_to_x():
        for n in range(1, Y):
            near_first(n).wait_recv()
        for n in [*range(1, X), 0]:
            at = x_at(n)
            total = rn[c, at, y].astype(F32)
            for m in range(1, Y):
                total += rn1[m, at].astype(F32)
            sn[at] = total.astype(BF)
            if n:
                near_second(n).start()

    def rz_copy(n):
        at = slot_there(n)
        return remote(zsend.at[tile_of(n)], zrecv.at[at], rz_s.at[n], rz_r.at[at], slot_device(n))

    def rz_arrival(n):
        return remote(zsend.at[tile_of(n)], zrecv.at[n], rz_s.at[n], rz_r.at[n], slot_device(n))

    half(0)
    dest_chunk(0)
    entity_over(1)
    dest_across(0)
    entity_on(2)
    dest_home(0)
    entity_over(2)
    half(1)
    dest_chunk(1)
    dest_chunk(2)
    for k in range(3):
        dwb[:, k * 128 : (k + 1) * 128] = jnp.transpose(dwf[k * 128 : (k + 1) * 128, :]).astype(BF)
    spread = one_hot(
        ((iota((128, 128), 1) & 15) == iota((128, 128), 0)) & (iota((128, 128), 1) < 16 * REL_DEV)
    )
    tail = nn(jnp.transpose(dwf[384:512, :]).astype(BF), spread)
    dwz[...] = jnp.where(slot_mask, tail, 0.0).astype(BF)
    for n in range(X):
        rel_far(cm, n)
        rc_far(n).start()
    for n in range(X):
        rel_near(cm, n)
    rc_near(0).start()
    for n in range(X):
        rel_far(c, n)
    far_to_plane()
    dest_across(1)
    dest_across(2)
    for n in range(X):
        rel_near(c, n)
    near_to_y()
    dest_home(1)
    dest_home(2)
    for k in range(CHUNKS):
        ent_copies[k].wait_send()
        entity_copy(k, rep, y_s, y_r, across).wait_send()
        entity_copy(k, rep, m_s, m_r, mate).wait_send()
        entity_copy(k, at_y, d_s, d_r, mate).wait_send()
    for n in range(X):
        far_core(n, c).wait_send()
    near_core(0, c).wait_send()
    for n in range(1, X):
        near_one(n, 0).wait_send()
        far_line(n, 0).wait_send()
    for n in range(1, Y):
        near_line(n, 0).wait_send()
        far_one(n, 0).wait_send()

    @pl.loop(1, Z)
    def _(n):
        tile_copy(n).wait_send()

    far_turn()
    near_to_x()

    ds_hi = dsf[...].astype(BF)
    ds_lo = (dsf[...] - ds_hi.astype(F32)).astype(BF)
    total = nt(ds_hi, ohs[...]) + nt(ds_lo, ohs[...])
    for h in range(HALVES):
        total += nn(ub[h], gs[h])
    sf[...] = total
    for k in range(CHUNKS):
        dc_copy(k).wait_send()
        dy_copy(k).wait_send()
    for n in range(X):
        rc_far(n).wait_send()
    rc_near(0).wait_send()
    for n in range(1, X):
        x_first(n).wait_send()
    for n in range(1, Y):
        y_first(n).wait_send()
        near_first(n).wait_send()

    total = sx[y].astype(F32)
    for n in range(1, Y):
        x_second(n).wait_recv()
        total += rx2[n].astype(F32)
    other = sy[x].astype(F32)
    for n in range(1, X):
        y_second(n).wait_recv()
        other += ry2[n].astype(F32)
    far_sum = jnp.concatenate([total, other], axis=0).astype(BF)
    shape = (SLOTS, FAR_ROWS)
    pick = one_hot(iota(shape, 1) == parts_of(iota(shape, 0))[1])
    tiles = nn(pick, far_sum)
    zsend[NEAR_Z * TILE :, :] = tiles[NEAR_Z * TILE :, :].astype(BF)

    @pl.loop(NEAR_Z, Z)
    def _(n):
        rz_copy(n).start()

    total = sn[x].astype(F32)
    for n in range(1, X):
        near_second(n).wait_recv()
        total += rn2[n].astype(F32)
    near_sum = total.astype(BF)
    shape = (NEAR_Z * TILE, NEAR_ROWS)
    pick = one_hot(iota(shape, 1) == parts_of(iota(shape, 0))[0])
    zsend[0 : NEAR_Z * TILE, :] = (nn(pick, near_sum) + tiles[0 : NEAR_Z * TILE, :]).astype(BF)

    @pl.loop(1, NEAR_Z)
    def _(n):
        rz_copy(n).start()

    for n in range(1, X):
        y_second(n).wait_send()
        near_second(n).wait_send()
    for n in range(1, Y):
        x_second(n).wait_send()
    for k in range(CHUNKS):
        dz_copy(k).wait_send()

    @pl.loop(1, Z)
    def _(n):
        rz_copy(n).wait_send()

    for k in range(CHUNKS):
        dz_copy(k).wait_recv()
    ent_grad[...] = sf[...] + ezr[...].astype(F32)

    def add_tile(n, acc):
        rz_arrival(n).wait_recv()
        return acc + zrecv[n].astype(F32)

    rel_grad[...] = lax.fori_loop(1, Z, add_tile, zsend[0:TILE, :].astype(F32))


def update(
    ent, state, rel, rel_state, ent_grad, rel_grad, new_ent, new_state, new_rel, new_rel_state
):
    grad = ent_grad[...]
    fresh = state[...] + jnp.sum(grad * grad, axis=0, keepdims=True) * (1.0 / D)
    new_state[...] = fresh
    new_ent[...] = ent[...] - grad * (0.5 / jnp.sqrt(fresh))

    lane = iota((REL_DEV, 128), 1)
    row5 = iota((REL_DEV, 128), 0)
    own_slot = lax.shift_right_logical(lane, 4) == row5
    ends = jnp.where(own_slot, jnp.broadcast_to(rel_grad[15:16, :], (REL_DEV, 128)), 0.0)
    fold_f = jnp.where(
        ((iota((128, 128), 0) & 15) == iota((128, 128), 1)) & (iota((128, 128), 0) < 16 * REL_DEV),
        1.0,
        0.0,
    )
    ends = jnp.dot(ends, fold_f, precision=lax.Precision.HIGHEST, preferred_element_type=F32)
    pieces = [rel_grad[k * REL_DEV : (k + 1) * REL_DEV, :] for k in range(3)] + [ends]
    squares = jnp.sum(sum(piece * piece for piece in pieces), axis=1, keepdims=True)
    eye = iota((REL_DEV, REL_DEV), 0) == iota((REL_DEV, REL_DEV), 1)
    old = jnp.broadcast_to(rel_state[...], (REL_DEV, REL_DEV))
    old = jnp.sum(jnp.where(eye, old, 0.0), axis=1, keepdims=True)
    fresh = old + squares * (1.0 / D)
    new_rel_state[...] = jnp.sum(
        jnp.where(eye, jnp.broadcast_to(fresh, (REL_DEV, REL_DEV)), 0.0), axis=0, keepdims=True
    )
    scale = 0.5 / jnp.sqrt(fresh)
    for k in range(3):
        at = slice(k * 128, (k + 1) * 128)
        new_rel[:, at] = rel[:, at] - pieces[k] * scale
    new_rel[:, 384:400] = rel[:, 384:400] - ends[:, 0:16] * scale


def scratch():
    vm = pltpu.VMEM
    dma = pltpu.SemaphoreType.DMA
    blocks = PI * CORES
    return [
        vm((D, ROWS), F32),
        vm((REL_DEV, D), F32),
        vm((1, EDGES), jnp.int32),
        vm((1, EDGES), jnp.int32),
        vm((1, EDGES), jnp.int32),
        vm((1, NEG), jnp.int32),
        vm((1, NEG), jnp.int32),
        vm((PAD, ROWS), BF),
        vm((REP, PAD, ROWS), BF),
        vm((SLOTS, 128), BF),
        vm((CORES, X, Y, NEAR_ROWS, 128), BF),
        vm((CORES, X, Y, FAR_ROWS, 128), BF),
        vm((TILE, 128), F32),
        vm((ROWS, EDGES), BF),
        vm((REP, ROWS, EDGES), BF),
        vm((CORES, PI * NR, EDGES), BF),
        vm((CORES, PI * FR, EDGES), BF),
        vm((CORES, PI * Z, EDGES), BF),
        vm((EDGES, blocks * NR), BF),
        vm((EDGES, blocks * FR), BF),
        vm((EDGES, blocks * Z), BF),
        vm((2, NEG_PAD), jnp.int32),
        vm((REP + 1, 16, ROWS), F32),
        vm((D, EDGES), F32),
        vm((PAD, EDGES), F32),
        vm((D, EDGES), F32),
        vm((PAD, EDGES), F32),
        vm((PAD, EDGES), F32),
        vm((D, EDGES), F32),
        vm((D, EDGES), F32),
        vm((D, EDGES), F32),
        vm((D, EDGES), F32),
        vm((PAD, EDGES), F32),
        vm((D, EDGES), BF),
        vm((EDGES, PAD), BF),
        vm((EDGES, PAD), BF),
        vm((REP, EDGES, ROWS), BF),
        vm((HALVES, EDGES, ROWS), BF),
        vm((HALVES, D, EDGES), BF),
        vm((HALVES, D, EDGES), BF),
        vm((HALVES, EDGES, ROWS), F32),
        vm((REP, EDGES, ROWS), F32),
        vm((EDGES, 384), BF),
        vm((EDGES, 128), BF),
        vm((CORES, YH, D, ROWS), BF),
        vm((YH, D, ROWS), BF),
        vm((D, ROWS), BF),
        vm((D, ROWS), BF),
        vm((D, ROWS), BF),
        vm((D, ROWS), BF),
        vm((CORES, X, Y, NEAR_ROWS, 128), BF),
        vm((CORES, X, Y, FAR_ROWS, 128), BF),
        vm((X, Y, NEAR_ROWS, 128), BF),
        vm((X, Y, FAR_ROWS, 128), BF),
        vm((Y, X, NEAR_ROWS, 128), BF),
        vm((X, NEAR_ROWS, 128), BF),
        vm((X, Y, FH, 128), BF),
        vm((Y, FH, 128), BF),
        vm((Y, X, FH, 128), BF),
        vm((X, FH, 128), BF),
        vm((X, NEAR_ROWS, 128), BF),
        vm((Y, FH, 128), BF),
        vm((X, FH, 128), BF),
        vm((SLOTS, 128), BF),
        vm((Z, TILE, 128), BF),
    ] + [
        dma((n,))
        for n in [Z] * 2 + [CHUNKS] * 8 + [max(X, Y)] * 12 + [CHUNKS] * 6 + [max(X, Y)] * 16 + [Z] * 2
    ] + [dma((7,))]


def local(
    entities, ent_state, relations, rel_state, src_rows, dst_rows, rel_ids, neg_src, neg_dst, edge_count
):
    vmem = pl.BlockSpec(memory_space=pltpu.VMEM)
    ent = entities.T
    ent_grad, rel_grad = pl.pallas_call(
        kernel,
        out_shape=(
            jax.ShapeDtypeStruct((D, ROWS), F32),
            jax.ShapeDtypeStruct((TILE, 128), F32),
        ),
        in_specs=[pl.BlockSpec(memory_space=pl.ANY)] * 7 + [vmem],
        out_specs=(vmem,) * 2,
        scratch_shapes=scratch(),
        compiler_params=pltpu.CompilerParams(
            collective_id=0, has_side_effects=True, vmem_limit_bytes=56 * 1024 * 1024
        ),
        name="bucket_round",
    )(
        ent, relations, src_rows, dst_rows, rel_ids, neg_src, neg_dst, edge_count.reshape(1, 1)
    )
    new_ent, new_state, new_rel, new_rel_state = pl.pallas_call(
        update,
        out_shape=(
            jax.ShapeDtypeStruct((D, ROWS), F32),
            jax.ShapeDtypeStruct((1, ROWS), F32),
            jax.ShapeDtypeStruct((REL_DEV, D), F32),
            jax.ShapeDtypeStruct((1, REL_DEV), F32),
        ),
        in_specs=[vmem] * 6,
        out_specs=(vmem,) * 4,
        name="row_update",
    )(
        ent,
        ent_state.reshape(1, ROWS),
        relations,
        rel_state.reshape(1, REL_DEV),
        ent_grad,
        rel_grad,
    )
    return (new_ent.T, new_state.reshape(ROWS), new_rel, new_rel_state.reshape(REL_DEV))


def solution(mesh):
    rows = P(("dom", "rep"), None)
    flat = P(("dom", "rep"))
    return jax.shard_map(
        local,
        mesh=mesh,
        in_specs=(rows, flat, rows, flat, rows, rows, rows, rows, rows, flat),
        out_specs=(rows, flat, rows, flat),
        check_vma=False,
    )
```
